32 devices in a mesh: groups: 2 (over x), tp: 4 (over y, core), dp: 4 (over z).
Axes of the slice: x: 2, y: 2, z: 4, core: 2. Of those that a mesh axis runs over, the one named last changes fastest.
Arguments:
- filter_feed_series: bfloat16 [4, 64, 8192], P(None, ('groups', 'dp'), 'tp'), parts along dimension 1, may hold values from -6 to 6
- valve_branch_series: bfloat16 [4, 64, 8192], P(None, ('groups', 'dp'), 'tp'), parts along dimension 1, may hold values from -6 to 6
- raw_increment_entries: bfloat16 [4, 64, 8192], P(None, ('groups', 'dp'), 'tp'), parts along dimension 1, may hold values from -6 to 6
- entering_memory_matrix: float32 [4, 64, 16], P(None, ('groups', 'dp')), parts along dimension 1, may hold values from -6 to 6
- leaving_memory_matrix: float32 [4, 64, 16], P(None, ('groups', 'dp')), parts along dimension 1, may hold values from -6 to 6
- emission_matrix: bfloat16 [8192, 4096], P('tp'), may hold values from -0.0625 to 0.0625
- recurrent_memory: float32 [8192, 1024], P('tp', ('groups', 'dp')), parts along dimension 1, may hold values from -6 to 6
- filter_recent_history: float32 [8192, 256], P('tp', ('groups', 'dp')), parts along dimension 1, may hold values from -6 to 6
- logarithmic_fading_speeds: float32 [8192, 16], replicated, may hold values from -2 to 2.7
- filter_coefficients: float32 [8192, 4], replicated, may hold values from -3 to 3
- filter_offset_term: float32 [8192], replicated, may hold values from -1 to 1
- increment_offset_term: float32 [8192], replicated, may hold values from -3 to 0.5
- residual_factor: float32 [8192], replicated, may hold values from 0.5 to 1.5
- remaining_ranks: int32 [3], replicated, may hold values from 0 to 3, as said below
- holder_segment_tallies: int32 [3], replicated, may hold values from 1 to 23, 64 in all
Outputs:
- decoded: bfloat16 [4, 64, 4096], P(None, ('groups', 'dp')), parts along dimension 1
- relocated_emission_matrix: bfloat16 [23552, 4096], P(('groups', 'tp')), parts along dimension 0
- relocated_recurrent_memory: float32 [11776, 1024], P('tp', ('groups', 'dp')), parts along dimension 1
- relocated_filter_history: float32 [11776, 256], P('tp', ('groups', 'dp')), parts along dimension 1
The draws below stay inside these ranges and needn't reach their ends.
There are 2 independent parts, one for each index of `groups`. The reference program is written for one: setup_inputs(seed, part) draws one part's arguments, and reference() takes and returns one part's arrays. A program takes and returns all parts, laid end to end along the dimension named above; an argument that names none is the same for every part. Nothing has to cross between parts.
Inputs may be any that keep to these rules, and one draw needn't show every extreme that they name: `remaining_ranks`: 3 distinct tp indices in increasing order; the first and the last index of tp are always among them. `holder_segment_tallies`: sums to 64; some owner has exactly 23 blocks.
All inputs are finite; a program needn't handle non-finite values.
Results may differ from the reference program's by a relative error of at most 0.008.
Values may be sent and summed in bfloat16 or wider, within the bound.
No kernel may reach another device: no remote copies, remote signals or barrier semaphores. Data moves between devices by JAX's collectives and lax.ppermute only.
A program may use at most 192 MiB of HBM per device.

```python
import math
import jax
import jax.numpy as jnp
import numpy as np

D = 4096
EXPANDED_WIDTH = 8192
LANE_MEMORY_DIM = 16
BLOCK = 128
STEPS = 4
COPY_PROMPTS = 32
NB = 64
NEW = 3
CAP = 23
N_TP = 4


def draw_remaining_ranks(key, part):
    key = jax.random.fold_in(key, 7)
    middle = jax.random.permutation(key, N_TP - 2)[:NEW - 2].astype(jnp.int32) + 1
    first = jnp.zeros((1,), jnp.int32)
    final = jnp.full((1,), N_TP - 1, jnp.int32)
    return jnp.sort(jnp.concatenate([first, middle, final])).astype(jnp.int32)


def steps_of(key, extent, pieces, smallest, high):
    level = 1.0
    for axis_at, blocks in pieces:
        heights = jax.random.uniform(jax.random.fold_in(jax.random.fold_in(key, 6), axis_at), (blocks,), jnp.float32, smallest / len(pieces), high / len(pieces))
        level = level * jnp.repeat(jnp.exp(heights), extent[axis_at] // blocks).reshape((-1,) + (1,) * (len(extent) - 1 - axis_at))
    return level


def split_up(amount, total, most, slope):
    weights = [(1 << 20) // math.isqrt(grade ** slope) + 1 for grade in range(2, amount + 1)]
    spare, given = total - most - (amount - 1), [1] * (amount - 1)
    while spare > 0:
        movable = [i for i in range(amount - 1) if given[i] < most]
        mass, left = sum([weights[i] for i in movable]), spare
        for i in movable:
            more = min(most - given[i], max(1, left * weights[i] // mass), spare)
            given[i] = given[i] + more
            spare = spare - more
    return np.array([most] + given)


def uneven_parts(stream_key, amount, total, reach, lean):
    if amount == 2:
        one = jax.random.randint(stream_key, (), max(1, total - reach), min(reach, total - 1) + 1)
        return jnp.stack([one, total - one])
    tallies = jnp.asarray(split_up(amount, total, reach, lean), jnp.int32)
    pairs = (amount - 1) // 2
    donor, sink = tallies[1:1 + 2 * pairs:2], tallies[2:2 + 2 * pairs:2]
    margin = jnp.minimum(donor - 1, reach - sink)
    passed = jax.random.randint(jax.random.fold_in(stream_key, 1), (pairs,), 0, 1 << 20) % (margin + 1)
    tallies = tallies.at[1:1 + 2 * pairs:2].set(donor - passed).at[2:2 + 2 * pairs:2].set(sink + passed)
    return tallies[jax.random.permutation(jax.random.fold_in(stream_key, 2), amount)]


def bell_draw(key, shape, width, most, split=(), kind=jnp.bfloat16):
    level = steps_of(key, shape, split, -0.22, 0.18) if split else 1.0
    array = jax.random.normal(key, shape, jnp.float32) * width * level
    return jnp.minimum(jnp.maximum(array, -most), most).astype(kind)


def setup_inputs(seed: int = 0, part: int = 0) -> dict:
    splits = jax.random.split(jax.random.key(seed), 16)
    part_keys = jax.random.split(jax.random.fold_in(splits[15], part), 16)
    filter_feed_series = bell_draw(part_keys[0], (STEPS, COPY_PROMPTS, EXPANDED_WIDTH), 1.0, 6.0, ((1, 4), (2, 4)))
    valve_branch_series = bell_draw(part_keys[1], (STEPS, COPY_PROMPTS, EXPANDED_WIDTH), 1.0, 6.0, ((1, 4), (2, 4)))
    raw_increment_entries = bell_draw(part_keys[2], (STEPS, COPY_PROMPTS, EXPANDED_WIDTH), 1.0, 6.0, ((1, 4), (2, 4)))
    entering_memory_matrix = bell_draw(part_keys[3], (STEPS, COPY_PROMPTS, LANE_MEMORY_DIM), 1.0, 6.0, ((1, 4),), jnp.float32)
    leaving_memory_matrix = bell_draw(part_keys[4], (STEPS, COPY_PROMPTS, LANE_MEMORY_DIM), 1.0, 6.0, ((1, 4),), jnp.float32)
    emission_matrix = bell_draw(splits[5], (EXPANDED_WIDTH, D), EXPANDED_WIDTH ** -0.5, 0.0625, ((0, 4),))
    recurrent_memory = bell_draw(part_keys[6], (EXPANDED_WIDTH, COPY_PROMPTS * LANE_MEMORY_DIM), 1.0, 6.0, ((0, 4), (1, 4)), jnp.float32)
    filter_recent_history = bell_draw(part_keys[7], (EXPANDED_WIDTH, COPY_PROMPTS * 4), 1.0, 6.0, ((0, 4), (1, 4)), jnp.float32)
    logarithmic_fading_speeds = jnp.clip(jax.random.uniform(splits[8], (EXPANDED_WIDTH, LANE_MEMORY_DIM), jnp.float32, -2.0, 2.7), -2.0, 2.7)
    filter_coefficients = bell_draw(splits[9], (EXPANDED_WIDTH, 4), 4 ** -0.5, 3.0, (), jnp.float32)
    filter_offset_term = jnp.clip(jax.random.uniform(splits[10], (EXPANDED_WIDTH,), jnp.float32, -1.0, 1.0), -1.0, 1.0)
    increment_offset_term = jnp.clip(jax.random.uniform(splits[11], (EXPANDED_WIDTH,), jnp.float32, -3.0, 0.5), -3.0, 0.5)
    residual_factor = jnp.clip(jax.random.uniform(splits[12], (EXPANDED_WIDTH,), jnp.float32, 0.5, 1.5), 0.5, 1.5)
    remaining_ranks = draw_remaining_ranks(jax.random.fold_in(splits[15], 71), part)
    holder_segment_tallies = uneven_parts(splits[14], NEW, NB, CAP, 2).astype(jnp.int32)
    return dict(filter_feed_series=filter_feed_series, valve_branch_series=valve_branch_series, raw_increment_entries=raw_increment_entries, entering_memory_matrix=entering_memory_matrix, leaving_memory_matrix=leaving_memory_matrix, emission_matrix=emission_matrix, recurrent_memory=recurrent_memory, filter_recent_history=filter_recent_history, logarithmic_fading_speeds=logarithmic_fading_speeds, filter_coefficients=filter_coefficients, filter_offset_term=filter_offset_term, increment_offset_term=increment_offset_term, residual_factor=residual_factor, remaining_ranks=remaining_ranks, holder_segment_tallies=holder_segment_tallies)


def redistribute_lanes(holder_directory, remaining_ranks, holder_segment_tallies):
    starts = jnp.cumsum(holder_segment_tallies) - holder_segment_tallies
    accelerator_roster = jnp.arange(N_TP, dtype=jnp.int32)
    corresponding_holder = (remaining_ranks[None, :] == accelerator_roster[:, None]).astype(jnp.int32)
    accelerator_first_lane = jnp.sum(corresponding_holder * starts[None, :], axis=1).astype(jnp.int32)
    accelerator_total = jnp.sum(corresponding_holder * holder_segment_tallies[None, :], axis=1).astype(jnp.int32)
    slot_rows = CAP * BLOCK
    rows = jnp.arange(N_TP * slot_rows, dtype=jnp.int32)
    owner = rows // slot_rows
    offset = rows % slot_rows
    valid = offset < accelerator_total[owner] * BLOCK
    source = jnp.where(valid, accelerator_first_lane[owner] * BLOCK + offset, 0).astype(jnp.int32)
    return jnp.where(valid[:, None], holder_directory[source], jnp.zeros((), holder_directory.dtype))


def reference(filter_feed_series, valve_branch_series, raw_increment_entries, entering_memory_matrix, leaving_memory_matrix, emission_matrix, recurrent_memory, filter_recent_history, logarithmic_fading_speeds, filter_coefficients, filter_offset_term, increment_offset_term, residual_factor, remaining_ranks, holder_segment_tallies):
    decay = -jnp.exp(logarithmic_fading_speeds)
    latent_entries = recurrent_memory.reshape(EXPANDED_WIDTH, COPY_PROMPTS, LANE_MEMORY_DIM)
    filter_recent_frame = filter_recent_history.reshape(EXPANDED_WIDTH, COPY_PROMPTS, 4)
    results = []
    for step in range(STEPS):
        x_now = filter_feed_series[step].astype(jnp.float32).T
        filter_recent_frame = jnp.concatenate([filter_recent_frame[:, :, 1:], x_now[:, :, None]], axis=2)
        inner = jax.nn.silu(jnp.sum(filter_recent_frame * filter_coefficients[:, None, :], axis=2) + filter_offset_term[:, None])
        delta = jax.nn.softplus(raw_increment_entries[step].astype(jnp.float32).T + increment_offset_term[:, None])
        latent_entries = jnp.exp(delta[:, :, None] * decay[:, None, :]) * latent_entries + (delta * inner)[:, :, None] * entering_memory_matrix[step][None, :, :]
        output_y = jnp.sum(latent_entries * leaving_memory_matrix[step][None, :, :], axis=2) + residual_factor[:, None] * inner
        gated = (output_y * jax.nn.silu(valve_branch_series[step].astype(jnp.float32).T)).astype(jnp.bfloat16)
        results.append(jnp.dot(gated.T, emission_matrix, preferred_element_type=jnp.float32).astype(jnp.bfloat16))
    decoded = jnp.stack(results, axis=0)
    relocated_emission_matrix = redistribute_lanes(emission_matrix, remaining_ranks, holder_segment_tallies)
    relocated_recurrent_memory = redistribute_lanes(latent_entries.reshape(EXPANDED_WIDTH, COPY_PROMPTS * LANE_MEMORY_DIM), remaining_ranks, holder_segment_tallies)
    relocated_filter_history = redistribute_lanes(filter_recent_frame.reshape(EXPANDED_WIDTH, COPY_PROMPTS * 4), remaining_ranks, holder_segment_tallies)
    return decoded, relocated_emission_matrix, relocated_recurrent_memory, relocated_filter_history
```

```python
import jax
import jax.numpy as jnp
from jax import lax
from jax.experimental import pallas as pl
from jax.experimental.pallas import tpu as pltpu
from jax.sharding import PartitionSpec as P

BLOCK = 128
UNIT = 16
BF = jnp.bfloat16
F32 = jnp.float32
AXES = ("groups", "tp", "dp")


def owner_ranges(remaining_ranks, holder_segment_tallies, holder_ranks):
    starts = jnp.cumsum(holder_segment_tallies) - holder_segment_tallies
    roster = jnp.arange(holder_ranks, dtype=jnp.int32)
    match = (remaining_ranks[None, :] == roster[:, None]).astype(jnp.int32)
    first = jnp.sum(match * starts[None, :], axis=1)
    total = jnp.sum(match * holder_segment_tallies[None, :], axis=1)
    return first, total


def pack_rows(columns, first, total, slot_rows):
    padded = jnp.pad(columns, ((0, slot_rows), (0, 0)))
    places = jnp.arange(slot_rows, dtype=jnp.int32)

    def one_owner(start, count):
        rows = lax.dynamic_slice_in_dim(padded, start * BLOCK, slot_rows, 0)
        return jnp.where((places < count * BLOCK)[:, None], rows, jnp.zeros_like(rows))

    packed = jax.vmap(one_owner)(first, total)
    return packed.reshape(-1, columns.shape[1])


def relocate_everywhere(rows, first, total, slot_rows):
    spread = lax.all_to_all(rows, "tp", split_axis=1, concat_axis=0, tiled=True)
    packed = pack_rows(spread, first, total, slot_rows)
    return lax.all_to_all(packed, "tp", split_axis=0, concat_axis=1, tiled=True)


def decode_plain(x, z, dt, enter, leave, ssm, conv, logs, taps, offs, inc, res, weights):
    steps, seqs, channels = x.shape
    h = ssm.reshape(channels, seqs, -1)
    window = conv.reshape(channels, seqs, 4)
    decay = -jnp.exp(logs)
    gated = []
    for step in range(steps):
        now = x[step].astype(F32).T
        window = jnp.concatenate([window[:, :, 1:], now[:, :, None]], axis=2)
        inner = jax.nn.silu(jnp.sum(window * taps[:, None, :], axis=2) + offs[:, None])
        delta = jax.nn.softplus(dt[step].astype(F32).T + inc[:, None])
        h = (
            jnp.exp(delta[:, :, None] * decay[:, None, :]) * h
            + (delta * inner)[:, :, None] * enter[step][None, :, :]
        )
        y = jnp.sum(h * leave[step][None, :, :], axis=2) + res[:, None] * inner
        gated.append((y * jax.nn.silu(z[step].astype(F32).T)).astype(BF))
    gated = jnp.concatenate(gated, axis=1)
    partial = lax.dot_general(
        gated, weights, (((0,), (0,)), ((), ())), preferred_element_type=F32
    )
    return partial, h.reshape(channels, -1), window.reshape(channels, -1)


def general(x, z, dt, enter, leave, w, ssm, conv, logs, taps, offs, inc, res, ranks, tallies):
    holders = lax.axis_size("tp")
    mine = lax.axis_index("tp")
    width, old = logs.shape[0], w.shape[0]
    slot_rows = (width // BLOCK // (holders * 3 // 4) + 2) * BLOCK
    first, total = owner_ranges(ranks, tallies, holders)

    def own(a):
        return lax.dynamic_slice_in_dim(a, mine * old, old, 0)

    moved_w = relocate_everywhere(w, first, total, slot_rows)
    partial, ssm, conv = decode_plain(
        x, z, dt, enter, leave, ssm, conv, own(logs), own(taps), own(offs), own(inc), own(res), w
    )
    decoded = lax.psum(partial, "tp").astype(BF).reshape(x.shape[0], x.shape[1], -1)
    return (
        decoded,
        moved_w,
        relocate_everywhere(ssm, first, total, slot_rows),
        relocate_everywhere(conv, first, total, slot_rows),
    )


CHUNK = 256


def decode_kernel(
    sc, x, z, dt, enter, leave, h0, hist, logs, taps, offs, inc, res, w,
    out_w, partial, states, ys, blank, own_sem, blank_sem,
):
    i = pl.program_id(0)
    steps, seqs, chunk = x.shape
    latents = logs.shape[0]
    per = chunk // BLOCK
    slots = out_w.shape[0] // BLOCK
    own_src, own_n, own_dst, filled = sc[1], sc[2], sc[3], sc[4]

    def blank_copy(b):
        return pltpu.make_async_copy(blank, out_w.at[pl.ds(b * BLOCK, BLOCK)], blank_sem.at[b])

    @pl.when(i == 0)
    def _():
        blank[...] = jnp.zeros_like(blank)
        partial[...] = jnp.zeros_like(partial)
        for b in range(slots):

            @pl.when(b >= filled)
            def _():
                blank_copy(b).start()

    def own_copy(j):
        at = jnp.clip(i * per + j - own_src + own_dst, 0, slots - 1)
        return pltpu.make_async_copy(
            w.at[pl.ds(j * BLOCK, BLOCK)],
            out_w.at[pl.ds(pl.multiple_of(at * BLOCK, BLOCK), BLOCK)],
            own_sem.at[j],
        )

    def is_own(j):
        b = i * per + j
        return (b >= own_src) & (b < own_src + own_n)

    for j in range(per):

        @pl.when(is_own(j))
        def _():
            own_copy(j).start()

    decay = -jnp.exp(logs[...])
    xs = [x[t].astype(F32) for t in range(steps)]
    window = [hist[k] for k in range(1, 4)] + xs
    tap = [taps[k : k + 1, :] for k in range(4)]
    inners, deltas, feeds = [], [], []
    for t in range(steps):
        mixed = offs[...] + sum(window[t + k] * tap[k] for k in range(4))
        inner = mixed / (1.0 + jnp.exp(-mixed))
        v = dt[t].astype(F32) + inc[...]
        delta = jnp.maximum(v, 0.0) + jnp.log1p(jnp.exp(-jnp.abs(v)))
        inners.append(inner)
        deltas.append(delta)
        feeds.append(delta * inner)
    turned = h0[...].T
    for s in range(seqs):
        h = turned[s * latents : (s + 1) * latents]
        for t in range(steps):
            c = t * seqs + s
            h = (
                jnp.exp(deltas[t][s : s + 1] * decay) * h
                + feeds[t][s : s + 1] * enter[:, c : c + 1]
            )
            ys[c : c + 1, :] = jnp.sum(h * leave[:, c : c + 1], axis=0, keepdims=True)
        states[s * latents : (s + 1) * latents, :] = h.astype(BF)
    states[seqs * latents :, :] = jnp.concatenate(xs, axis=0).astype(BF)
    gated = []
    for t in range(steps):
        y = ys[t * seqs : (t + 1) * seqs, :] + res[...] * inners[t]
        g = z[t].astype(F32)
        gated.append(y * (g / (1.0 + jnp.exp(-g))))
    gated = jnp.concatenate(gated, axis=0).astype(BF)
    partial[...] += jnp.dot(gated, w[...], preferred_element_type=F32)

    for j in range(per):

        @pl.when(is_own(j))
        def _():
            own_copy(j).wait()

    @pl.when(i == pl.num_programs(0) - 1)
    def _():
        for b in range(slots):

            @pl.when(b >= filled)
            def _():
                blank_copy(b).wait()


def decode_here(scalars, slots, x, z, dt, enter, leave, w, ssm, conv, logs, taps, offs, inc, res):
    steps, seqs, channels = x.shape
    latents = logs.shape[1]
    features = w.shape[1]
    n = channels // CHUNK
    series = pl.BlockSpec((steps, seqs, CHUNK), lambda i, sc: (0, 0, i))
    small = pl.BlockSpec((latents, steps * seqs), lambda i, sc: (0, 0))

    def lanes(rows):
        return pl.BlockSpec((rows, CHUNK), lambda i, sc: (0, sc[0] * n + i))

    grid_spec = pltpu.PrefetchScalarGridSpec(
        num_scalar_prefetch=1,
        grid=(n,),
        in_specs=[
            series, series, series, small, small,
            pl.BlockSpec((CHUNK, seqs * latents), lambda i, sc: (i, 0)),
            pl.BlockSpec((4, seqs, CHUNK), lambda i, sc: (0, 0, i)),
            lanes(latents), lanes(4), lanes(1), lanes(1), lanes(1),
            pl.BlockSpec((CHUNK, features), lambda i, sc: (i, 0)),
        ],
        out_specs=[
            pl.BlockSpec(memory_space=pl.ANY),
            pl.BlockSpec((steps * seqs, features), lambda i, sc: (0, 0)),
            pl.BlockSpec((seqs * (latents + 4), CHUNK), lambda i, sc: (0, i)),
        ],
        scratch_shapes=[
            pltpu.VMEM((steps * seqs, CHUNK), F32),
            pltpu.VMEM((BLOCK, features), BF),
            pltpu.SemaphoreType.DMA((CHUNK // BLOCK,)),
            pltpu.SemaphoreType.DMA((slots,)),
        ],
    )
    rows = steps * seqs
    return pl.pallas_call(
        decode_kernel,
        grid_spec=grid_spec,
        out_shape=(
            jax.ShapeDtypeStruct((slots * BLOCK, features), BF),
            jax.ShapeDtypeStruct((rows, features), F32),
            jax.ShapeDtypeStruct((seqs * (latents + 4), channels), BF),
        ),
        compiler_params=pltpu.CompilerParams(vmem_limit_bytes=24 << 20),
        cost_estimate=pl.CostEstimate(
            flops=2 * rows * channels * features,
            bytes_accessed=2 * 2 * channels * features,
            transcendentals=rows * channels * latents,
        ),
        name="decode",
    )(
        scalars, x, z, dt,
        enter.transpose(2, 0, 1).reshape(latents, rows),
        leave.transpose(2, 0, 1).reshape(latents, rows),
        ssm, conv.T.reshape(seqs, 4, channels).transpose(1, 0, 2), logs.T, taps.T,
        offs.reshape(1, -1), inc.reshape(1, -1), res.reshape(1, -1), w,
    )


def place_rows(scalars, out_w, pieces, side=None):
    slots = out_w.shape[0] // BLOCK
    n = len(pieces)
    arrays = []
    for piece in pieces:
        if not any(piece[0] is a for a in arrays):
            arrays.append(piece[0])
    which = [next(k for k, a in enumerate(arrays) if a is piece[0]) for piece in pieces]
    shapes = [piece[1:] for piece in pieces]
    side_n = 0 if side is None else side.shape[0] // BLOCK
    operands = arrays + ([] if side is None else [side])

    def kernel(sc, *refs):
        ins, out = refs[: len(operands)], refs[len(operands) + 1]
        sems, side_sems = refs[-2], refs[-1]
        recv, row0, q = sc[5], sc[6], sc[7]
        c_src, c_n, c_dst = sc[8], sc[9], sc[10]

        def copies():
            for k, (first, rows, offset) in enumerate(shapes):
                at = jnp.clip(row0 + offset(q) * UNIT, 0, slots * BLOCK - rows)
                yield pltpu.make_async_copy(
                    ins[which[k]].at[pl.ds(first, rows)],
                    out.at[pl.ds(pl.multiple_of(at, UNIT), rows)],
                    sems.at[k],
                )

        def side_copy(b):
            src = jnp.clip(c_src + b, 0, side_n - 1) * BLOCK
            dst = jnp.clip(c_dst + b, 0, slots - 1) * BLOCK
            return pltpu.make_async_copy(
                ins[-1].at[pl.ds(pl.multiple_of(src, BLOCK), BLOCK)],
                out.at[pl.ds(pl.multiple_of(dst, BLOCK), BLOCK)],
                side_sems.at[b],
            )

        @pl.when(recv == 1)
        def _():
            for copy in copies():
                copy.start()

        for b in range(side_n):

            @pl.when(b < c_n)
            def _():
                side_copy(b).start()

        @pl.when(recv == 1)
        def _():
            for copy in copies():
                copy.wait()

        for b in range(side_n):

            @pl.when(b < c_n)
            def _():
                side_copy(b).wait()

    any_spec = pl.BlockSpec(memory_space=pl.ANY)
    moved = sum(s[1] for s in shapes) * out_w.shape[1] * 4
    return pl.pallas_call(
        kernel,
        grid_spec=pltpu.PrefetchScalarGridSpec(
            num_scalar_prefetch=1,
            grid=(),
            in_specs=[any_spec] * (len(operands) + 1),
            out_specs=any_spec,
            scratch_shapes=[
                pltpu.SemaphoreType.DMA((n,)),
                pltpu.SemaphoreType.DMA((max(side_n, 1),)),
            ],
        ),
        out_shape=jax.ShapeDtypeStruct(out_w.shape, out_w.dtype),
        input_output_aliases={len(operands) + 1: 0},
        cost_estimate=pl.CostEstimate(flops=0, bytes_accessed=moved, transcendentals=0),
        name="place_rows",
    )(scalars, *operands, out_w)


def place_states(scalars, slots, own, side, across, latent_rows):
    rows = own.shape[0]
    seqs = (rows - latent_rows) // 4

    def kernel(sc, own_ref, side_ref, across_ref, ssm, conv, turned):
        own_src, own_n, own_dst, filled = sc[1], sc[2], sc[3], sc[4]
        recv, recv_dst = sc[5], sc[6] // BLOCK
        c_src, c_n, c_dst = sc[8], sc[9], sc[10]

        def put(b, ref, at):
            block = ref[:, pl.ds(pl.multiple_of(at * BLOCK, BLOCK), BLOCK)].astype(F32)
            ssm[b * BLOCK : (b + 1) * BLOCK, :] = block[:latent_rows].T
            for k in range(4):
                at = latent_rows + k * seqs
                turned[pl.ds(k, seqs, stride=4), :] = block[at : at + seqs]
            conv[:, b * BLOCK : (b + 1) * BLOCK] = turned[...]

        across_n = across_ref.shape[1] // BLOCK
        for b in range(slots):
            in_own = (b >= own_dst) & (b < own_dst + own_n)
            in_side = (b >= c_dst) & (b < c_dst + c_n)
            in_across = (recv == 1) & (b >= recv_dst) & (b < recv_dst + across_n)

            @pl.when(in_own)
            def _():
                put(b, own_ref, b - own_dst + own_src)

            @pl.when(in_side)
            def _():
                put(b, side_ref, b - c_dst + c_src)

            @pl.when(in_across)
            def _():
                put(b, across_ref, b - recv_dst)

            @pl.when(b >= filled)
            def _():
                ssm[b * BLOCK : (b + 1) * BLOCK, :] = jnp.zeros((BLOCK, latent_rows), F32)
                conv[:, b * BLOCK : (b + 1) * BLOCK] = jnp.zeros((rows - latent_rows, BLOCK), F32)

    vmem = pl.BlockSpec(memory_space=pltpu.VMEM)
    return pl.pallas_call(
        kernel,
        grid_spec=pltpu.PrefetchScalarGridSpec(
            num_scalar_prefetch=1,
            grid=(),
            in_specs=[vmem] * 3,
            out_specs=[vmem] * 2,
            scratch_shapes=[pltpu.VMEM((rows - latent_rows, BLOCK), F32)],
        ),
        out_shape=(
            jax.ShapeDtypeStruct((slots * BLOCK, latent_rows), F32),
            jax.ShapeDtypeStruct((rows - latent_rows, slots * BLOCK), F32),
        ),
        compiler_params=pltpu.CompilerParams(vmem_limit_bytes=24 << 20),
        name="place_states",
    )(scalars, own, side, across)


def neighbours(x, z, dt, enter, leave, w, ssm, conv, logs, taps, offs, inc, res, ranks, tallies):
    groups, depth = lax.axis_size("groups"), lax.axis_size("dp")
    g, t, d = (lax.axis_index(a) for a in AXES)
    old_blocks = w.shape[0] // BLOCK
    cap = (logs.shape[0] // BLOCK) // 3 + 2
    most = cap - old_blocks
    half = 2 * old_blocks

    def place(a, b, c):
        return (a * 4 + b) * depth + c

    every = [(a, c) for a in range(groups) for c in range(depth)]
    across = [(place(a, u, c), place(a, 3 - u, c)) for a, c in every for u in (1, 2)]
    along_x = [(place(a, u, c), place(1 - a, u, c)) for a, c in every for u in (1, 2)]
    along_z = [(place(a, u, c), place(a, u, c ^ 1)) for a, c in every for u in (1, 2)]
    inside = [(place(a, u, c), place(a, v, c)) for a, c in every for u, v in ((1, 0), (2, 3))]
    cores = [(place(a, u, c), place(a, u ^ 1, c)) for a, c in every for u in range(4)]
    chips = [(place(a, u, c), place(a, u ^ 2, c)) for a, c in every for u in range(4)]

    q = 2 * g + (d & 1)
    middle = ranks[1]
    t0, t1, t2 = tallies[0], tallies[1], tallies[2]
    is_mid = (t == middle).astype(jnp.int32)
    crossing = jnp.where(middle == 2, half - t0, half - t2)

    def by_rank(first, low, high, last):
        return jnp.where(t == 0, first, jnp.where(t == 3, last, jnp.where(t == 1, low, high)))

    own_src = by_rank(0, t0 - old_blocks, 0, 0)
    own_n = by_rank(old_blocks, is_mid * (half - t0), is_mid * (half - t2), old_blocks)
    own_dst = by_rank(0, 0, crossing, t2 - old_blocks)
    filled = by_rank(t0, is_mid * t1, is_mid * t1, t2)
    row0 = by_rank(0, (half - t0) * BLOCK, 0, 0)
    c_src = by_rank(0, 0, 0, most - (t2 - old_blocks))
    c_n = by_rank(t0 - old_blocks, 0, 0, t2 - old_blocks)
    c_dst = by_rank(old_blocks, 0, 0, 0)
    scalars = jnp.stack(
        [t, own_src, own_n, own_dst, filled, is_mid, row0, q, c_src, c_n, c_dst]
    ).astype(jnp.int32)

    def permute(a, pairs):
        return lax.ppermute(a, AXES, pairs)

    def body(v, args):
        scalars, x, z, dt, enter, leave, w, ssm, conv, logs, taps, offs, inc, res = args
        part = v
        relay = v // 2
        base = jnp.where(t == 1, (old_blocks - v) * BLOCK, 0)

        def cut(unit, units):
            return lax.dynamic_slice_in_dim(w, base + unit * UNIT, units * UNIT, 0)

        far = 3 - q
        near_x, near_z = q ^ 2, q ^ 1
        y1 = permute(cut(2 * part * q, part), across)
        side_w = lax.dynamic_slice_in_dim(
            w, jnp.where(t == 1, 0, (old_blocks - most) * BLOCK), most * BLOCK, 0
        )
        side = permute(side_w, inside)
        out_w, partial, states = decode_here(
            scalars, cap, x, z, dt, enter, leave, w, ssm, conv, logs, taps, offs, inc, res
        )
        y2 = permute(cut(2 * part * q + part, part), across)
        x1, z1 = permute(y1, along_x), permute(y1, along_z)
        y3 = permute(cut(2 * part * far + 2 * relay, 2 * part - 2 * relay), across)
        x2 = permute(jnp.concatenate([y2, z1[: relay * UNIT]]), along_x)
        z2 = permute(jnp.concatenate([y2, x1[relay * UNIT : 2 * relay * UNIT]]), along_z)

        features = partial.shape[1]
        core = (t & 1) * (features // 2)
        mine = lax.dynamic_slice_in_dim(partial, core, features // 2, 1)
        theirs = lax.dynamic_slice_in_dim(partial, features // 2 - core, features // 2, 1)
        chip_sum = (mine + permute(theirs, cores)).astype(BF)
        total = (chip_sum.astype(F32) + permute(chip_sum, chips).astype(F32)).astype(BF)
        other = permute(total, cores)
        low = (t & 1) == 0
        decoded = jnp.concatenate(
            [jnp.where(low, total, other), jnp.where(low, other, total)], axis=1
        )

        rows = states.shape[0]
        side_s = permute(
            lax.dynamic_slice_in_dim(
                states, jnp.where(t == 1, 0, (old_blocks - most) * BLOCK), most * BLOCK, 1
            ),
            inside,
        )
        across_s = permute(
            lax.dynamic_slice_in_dim(states, base, v * BLOCK, 1), across
        )
        n = part * UNIT
        out_w = place_rows(
            scalars,
            out_w,
            [
                (y1, 0, n, lambda q: 2 * part * q),
                (x1, 0, n, lambda q: 2 * part * (q ^ 2)),
                (z1, 0, n, lambda q: 2 * part * (q ^ 1)),
            ],
            side,
        )
        m = relay * UNIT
        out_w = place_rows(
            scalars,
            out_w,
            [
                (y2, 0, n, lambda q: 2 * part * q + part),
                (x2, 0, n, lambda q: 2 * part * (q ^ 2) + part),
                (z2, 0, n, lambda q: 2 * part * (q ^ 1) + part),
                (x2, n, m, lambda q: 2 * part * (3 - q)),
                (z2, n, m, lambda q: 2 * part * (3 - q) + relay),
                (y3, 0, 2 * n - 2 * m, lambda q: 2 * part * (3 - q) + 2 * relay),
            ],
        )
        latent_rows = ssm.shape[1]
        new_ssm, new_conv = place_states(scalars, cap, states, side_s, across_s, latent_rows)
        return decoded, out_w, new_ssm, new_conv

    args = (scalars, x, z, dt, enter, leave, w, ssm, conv, logs, taps, offs, inc, res)
    fewest = half - cap
    branches = [lambda args, v=v: body(v, args) for v in range(fewest, old_blocks - 1)]
    decoded, out_w, new_ssm, new_conv = lax.switch(crossing - fewest, branches, args)
    return decoded.reshape(x.shape[0], x.shape[1], -1), out_w, new_ssm, new_conv.T


def solution(mesh):
    placed = (
        P(None, ("groups", "dp"), "tp"),
        P(None, ("groups", "dp"), "tp"),
        P(None, ("groups", "dp"), "tp"),
        P(None, ("groups", "dp"), None),
        P(None, ("groups", "dp"), None),
        P("tp", None),
        P("tp", ("groups", "dp")),
        P("tp", ("groups", "dp")),
    ) + (P(),) * 7
    square = mesh.shape["tp"] == 4 and mesh.shape["groups"] == 2 and mesh.shape["dp"] % 2 == 0
    return jax.shard_map(
        neighbours if square else general,
        mesh=mesh,
        in_specs=placed,
        out_specs=(
            P(None, ("groups", "dp"), None),
            P(("groups", "tp"), None),
            P("tp", ("groups", "dp")),
            P("tp", ("groups", "dp")),
        ),
        check_vma=False,
    )
```

```python
import jax
import jax.numpy as jnp
from jax import lax
from jax.experimental import pallas as pl
from jax.experimental.pallas import tpu as pltpu
from jax.sharding import PartitionSpec as P

BLOCK = 128
UNIT = 16
BF = jnp.bfloat16
F32 = jnp.float32
AXES = ("groups", "tp", "dp")


def owner_ranges(remaining_ranks, holder_segment_tallies, holder_ranks):
    starts = jnp.cumsum(holder_segment_tallies) - holder_segment_tallies
    roster = jnp.arange(holder_ranks, dtype=jnp.int32)
    match = (remaining_ranks[None, :] == roster[:, None]).astype(jnp.int32)
    first = jnp.sum(match * starts[None, :], axis=1)
    total = jnp.sum(match * holder_segment_tallies[None, :], axis=1)
    return first, total


def pack_rows(columns, first, total, slot_rows):
    padded = jnp.pad(columns, ((0, slot_rows), (0, 0)))
    places = jnp.arange(slot_rows, dtype=jnp.int32)

    def one_owner(start, count):
        rows = lax.dynamic_slice_in_dim(padded, start * BLOCK, slot_rows, 0)
        return jnp.where((places < count * BLOCK)[:, None], rows, jnp.zeros_like(rows))

    packed = jax.vmap(one_owner)(first, total)
    return packed.reshape(-1, columns.shape[1])


def relocate_everywhere(rows, first, total, slot_rows):
    spread = lax.all_to_all(rows, "tp", split_axis=1, concat_axis=0, tiled=True)
    packed = pack_rows(spread, first, total, slot_rows)
    return lax.all_to_all(packed, "tp", split_axis=0, concat_axis=1, tiled=True)


def decode_plain(x, z, dt, enter, leave, ssm, conv, logs, taps, offs, inc, res, weights):
    steps, seqs, channels = x.shape
    h = ssm.reshape(channels, seqs, -1)
    window = conv.reshape(channels, seqs, 4)
    decay = -jnp.exp(logs)
    gated = []
    for step in range(steps):
        now = x[step].astype(F32).T
        window = jnp.concatenate([window[:, :, 1:], now[:, :, None]], axis=2)
        inner = jax.nn.silu(jnp.sum(window * taps[:, None, :], axis=2) + offs[:, None])
        delta = jax.nn.softplus(dt[step].astype(F32).T + inc[:, None])
        h = (
            jnp.exp(delta[:, :, None] * decay[:, None, :]) * h
            + (delta * inner)[:, :, None] * enter[step][None, :, :]
        )
        y = jnp.sum(h * leave[step][None, :, :], axis=2) + res[:, None] * inner
        gated.append((y * jax.nn.silu(z[step].astype(F32).T)).astype(BF))
    gated = jnp.concatenate(gated, axis=1)
    partial = lax.dot_general(
        gated, weights, (((0,), (0,)), ((), ())), preferred_element_type=F32
    )
    return partial, h.reshape(channels, -1), window.reshape(channels, -1)


def general(x, z, dt, enter, leave, w, ssm, conv, logs, taps, offs, inc, res, ranks, tallies):
    holders = lax.axis_size("tp")
    mine = lax.axis_index("tp")
    width, old = logs.shape[0], w.shape[0]
    slot_rows = (width // BLOCK // (holders * 3 // 4) + 2) * BLOCK
    first, total = owner_ranges(ranks, tallies, holders)

    def own(a):
        return lax.dynamic_slice_in_dim(a, mine * old, old, 0)

    moved_w = relocate_everywhere(w, first, total, slot_rows)
    partial, ssm, conv = decode_plain(
        x, z, dt, enter, leave, ssm, conv, own(logs), own(taps), own(offs), own(inc), own(res), w
    )
    decoded = lax.psum(partial, "tp").astype(BF).reshape(x.shape[0], x.shape[1], -1)
    return (
        decoded,
        moved_w,
        relocate_everywhere(ssm, first, total, slot_rows),
        relocate_everywhere(conv, first, total, slot_rows),
    )


def each(low, high, act):
    lax.fori_loop(low, high, lambda b, _: (act(b), 0)[1], 0)


CHUNK = 256
WIDE = 2048


def decode_kernel(
    sc, x, z, dt, enter, leave, h0, hist, logs, taps, offs, inc, res, w_all,
    out_w, side, second, third, partial, states, ys, deltas, feeds, turned, w, w_sem, own_sem, side_sem, cut_sem,
):
    i = pl.program_id(0)
    steps, seqs, chunk = x.shape
    latents = logs.shape[0]
    per = chunk // BLOCK
    blocks = w_all.shape[0] // BLOCK
    slots = out_w.shape[0] // BLOCK
    side_n = side.shape[0] // BLOCK
    own_src, own_n, own_dst, side_src = sc[1], sc[2], sc[3], sc[11]

    def rows(b):
        return pl.ds(pl.multiple_of(b * BLOCK, BLOCK), BLOCK)

    def fetch(b):
        return pltpu.make_async_copy(w_all.at[rows(b)], w.at[rows(b)], w_sem.at[b])

    def keep(b):
        at = jnp.clip(b - own_src + own_dst, 0, slots - 1)
        return pltpu.make_async_copy(w.at[rows(b)], out_w.at[rows(at)], own_sem.at[b])

    def pass_on(b):
        at = jnp.clip(b - side_src, 0, side_n - 1)
        return pltpu.make_async_copy(w.at[rows(b)], side.at[rows(at)], side_sem.at[b])

    @pl.when(i == 0)
    def _():
        each(0, blocks, lambda b: fetch(b).start())
        partial[...] = jnp.zeros_like(partial)

    decay = -jnp.exp(logs[...])
    xs = [x[t].astype(F32) for t in range(steps)]
    window = [hist[k] for k in range(1, 4)] + xs
    tap = [taps[k : k + 1, :] for k in range(4)]
    inners = []
    for t in range(steps):
        mixed = offs[...] + sum(window[t + k] * tap[k] for k in range(4))
        inner = mixed / (1.0 + jnp.exp(-mixed))
        v = dt[t].astype(F32) + inc[...]
        delta = jnp.maximum(v, 0.0) + jnp.log1p(jnp.exp(-jnp.abs(v)))
        inners.append(inner)
        deltas[t * seqs : (t + 1) * seqs, :] = delta
        feeds[t * seqs : (t + 1) * seqs, :] = delta * inner
    turned[...] = h0[...].T

    def wide(a):
        return jnp.concatenate([a] * per, axis=1)

    def sequence(s, _):
        at = pl.ds(pl.multiple_of(s * latents, latents), latents)
        h = turned[at, :]
        for t in range(steps):
            c = t * seqs + s
            row = pl.ds(c, 1)
            h = jnp.exp(deltas[row, :] * decay) * h + feeds[row, :] * wide(enter[c])
            ys[row, :] = jnp.sum(h * wide(leave[c]), axis=0, keepdims=True)
        states[at, :] = h.astype(BF)
        return 0

    lax.fori_loop(0, seqs, sequence, 0)
    states[seqs * latents :, :] = jnp.concatenate(xs, axis=0).astype(BF)
    gated = []
    for t in range(steps):
        y = ys[t * seqs : (t + 1) * seqs, :] + res[...] * inners[t]
        g = z[t].astype(F32)
        gated.append(y * (g / (1.0 + jnp.exp(-g))))
    gated = jnp.concatenate(gated, axis=0).astype(BF)

    def arrived(j, _):
        b = i * per + j
        fetch(b).wait()

        @pl.when((b >= own_src) & (b < own_src + own_n))
        def _():
            keep(b).start()

        @pl.when((b >= side_src) & (b < side_src + side_n))
        def _():
            pass_on(b).start()

        return 0

    lax.fori_loop(0, per, arrived, 0)
    last = i == pl.num_programs(0) - 1
    cuts = [
        pltpu.make_async_copy(
            w.at[pl.ds(pl.multiple_of(sc[row], UNIT), to.shape[0])], to, cut_sem.at[k]
        )
        for k, (row, to) in enumerate(((13, second), (14, third)))
    ]

    @pl.when(last)
    def _():
        for copy in cuts:
            copy.start()

    here = pl.ds(pl.multiple_of(i * chunk, chunk), chunk)

    def project(k):
        cols = pl.ds(pl.multiple_of(k * WIDE, WIDE), WIDE)
        partial[:, cols] += jnp.dot(gated, w[here, cols], preferred_element_type=F32)

    each(0, partial.shape[1] // WIDE, project)

    @pl.when(last)
    def _():
        for copy in cuts:
            copy.wait()
        each(own_src, own_src + own_n, lambda b: keep(b).wait())
        each(side_src, jnp.minimum(side_src + side_n, blocks), lambda b: pass_on(b).wait())


def decode_here(scalars, slots, side_n, cut_rows, x, z, dt, enter, leave, w, ssm, conv, logs, taps, offs, inc, res):
    steps, seqs, channels = x.shape
    latents = logs.shape[1]
    features = w.shape[1]
    n = channels // CHUNK
    series = pl.BlockSpec((steps, seqs, CHUNK), lambda i, sc: (0, 0, i))
    small = pl.BlockSpec((steps * seqs, latents, BLOCK), lambda i, sc: (0, 0, 0))

    def lanes(rows):
        return pl.BlockSpec((rows, CHUNK), lambda i, sc: (0, sc[0] * n + i))

    grid_spec = pltpu.PrefetchScalarGridSpec(
        num_scalar_prefetch=1,
        grid=(n,),
        in_specs=[
            series, series, series, small, small,
            pl.BlockSpec((CHUNK, seqs * latents), lambda i, sc: (i, 0)),
            pl.BlockSpec((4, seqs, CHUNK), lambda i, sc: (0, 0, i)),
            lanes(latents), lanes(4), lanes(1), lanes(1), lanes(1),
            pl.BlockSpec(memory_space=pltpu.HBM),
        ],
        out_specs=[
            pl.BlockSpec(memory_space=pl.ANY),
            pl.BlockSpec(memory_space=pl.ANY),
            pl.BlockSpec(memory_space=pl.ANY),
            pl.BlockSpec(memory_space=pl.ANY),
            pl.BlockSpec((steps * seqs, features), lambda i, sc: (0, 0)),
            pl.BlockSpec((seqs * (latents + 4), CHUNK), lambda i, sc: (0, i)),
        ],
        scratch_shapes=[
            pltpu.VMEM((steps * seqs, CHUNK), F32),
            pltpu.VMEM((steps * seqs, CHUNK), F32),
            pltpu.VMEM((steps * seqs, CHUNK), F32),
            pltpu.VMEM((seqs * latents, CHUNK), F32),
            pltpu.VMEM((channels, features), BF),
            pltpu.SemaphoreType.DMA((channels // BLOCK,)),
            pltpu.SemaphoreType.DMA((channels // BLOCK,)),
            pltpu.SemaphoreType.DMA((channels // BLOCK,)),
            pltpu.SemaphoreType.DMA((2,)),
        ],
    )
    rows = steps * seqs
    return pl.pallas_call(
        decode_kernel,
        grid_spec=grid_spec,
        out_shape=(
            jax.ShapeDtypeStruct((slots * BLOCK, features), BF),
            jax.ShapeDtypeStruct((side_n * BLOCK, features), BF),
            jax.ShapeDtypeStruct((cut_rows[0], features), BF),
            jax.ShapeDtypeStruct((cut_rows[1], features), BF),
            jax.ShapeDtypeStruct((rows, features), F32),
            jax.ShapeDtypeStruct((seqs * (latents + 4), channels), BF),
        ),
        compiler_params=pltpu.CompilerParams(vmem_limit_bytes=26 << 20),
        cost_estimate=HINT,
        name="decode",
    )(
        scalars, x, z, dt,
        jnp.broadcast_to(enter.reshape(rows, latents, 1), (rows, latents, BLOCK)),
        jnp.broadcast_to(leave.reshape(rows, latents, 1), (rows, latents, BLOCK)),
        ssm, conv.T.reshape(seqs, 4, channels).transpose(1, 0, 2), logs.T, taps.T,
        offs.reshape(1, -1), inc.reshape(1, -1), res.reshape(1, -1), w,
    )


HINT = pl.CostEstimate(flops=0, bytes_accessed=1024, transcendentals=0)


def cut_rows(scalars, w, rows):
    def kernel(sc, w_ref, out, sem):
        copy = pltpu.make_async_copy(
            w_ref.at[pl.ds(pl.multiple_of(sc[12], UNIT), rows)], out, sem
        )
        copy.start()
        copy.wait()

    return pl.pallas_call(
        kernel,
        grid_spec=pltpu.PrefetchScalarGridSpec(
            num_scalar_prefetch=1,
            grid=(),
            in_specs=[pl.BlockSpec(memory_space=pltpu.HBM)],
            out_specs=pl.BlockSpec(memory_space=pltpu.VMEM),
            scratch_shapes=[pltpu.SemaphoreType.DMA],
        ),
        out_shape=jax.ShapeDtypeStruct((rows, w.shape[1]), w.dtype),
        compiler_params=pltpu.CompilerParams(vmem_limit_bytes=8 << 20),
        cost_estimate=HINT,
        name="cut_rows",
    )(scalars, w)


def place_rows(scalars, out_w, pieces, side=None):
    slots, features = out_w.shape[0] // BLOCK, out_w.shape[1]
    arrays = []
    for piece in pieces:
        if not any(piece[0] is a for a in arrays):
            arrays.append(piece[0])
    jobs = []
    for array, first, rows, offset in pieces:
        jobs.append((next(k for k, a in enumerate(arrays) if a is array), first, rows, offset))
    side_n = 0 if side is None else side.shape[0] // BLOCK
    operands = arrays + ([] if side is None else [side])
    staged = sum(job[2] for job in jobs)

    def kernel(sc, *refs):
        ins, out = refs[: len(operands)], refs[len(operands) + 1]
        stage, side_stage, sems, side_sems, blank, blank_sems = refs[len(operands) + 2 :]
        recv, row0, q = sc[5], sc[6], sc[7]
        c_src, c_n, c_dst = sc[8], sc[9], sc[10]
        starts = [sum(job[2] for job in jobs[:k]) for k in range(len(jobs))]

        def fetch(k):
            which, first, rows, _ = jobs[k]
            return pltpu.make_async_copy(
                ins[which].at[pl.ds(first, rows)],
                stage.at[pl.ds(starts[k], rows)],
                sems.at[2 * k],
            )

        def store(k):
            _, _, rows, offset = jobs[k]
            row = jnp.clip(row0 + offset(q) * UNIT, 0, slots * BLOCK - rows)
            return pltpu.make_async_copy(
                stage.at[pl.ds(starts[k], rows)],
                out.at[pl.ds(pl.multiple_of(row, UNIT), rows)],
                sems.at[2 * k + 1],
            )

        def side_fetch(b):
            src = jnp.clip(c_src + b, 0, side_n - 1) * BLOCK
            return pltpu.make_async_copy(
                ins[-1].at[pl.ds(pl.multiple_of(src, BLOCK), BLOCK)],
                side_stage.at[pl.ds(pl.multiple_of(b * BLOCK, BLOCK), BLOCK)],
                side_sems.at[2 * b],
            )

        def side_store(b):
            dst = jnp.clip(c_dst + b, 0, slots - 1) * BLOCK
            return pltpu.make_async_copy(
                side_stage.at[pl.ds(pl.multiple_of(b * BLOCK, BLOCK), BLOCK)],
                out.at[pl.ds(pl.multiple_of(dst, BLOCK), BLOCK)],
                side_sems.at[2 * b + 1],
            )

        def clear(b):
            return pltpu.make_async_copy(
                blank, out.at[pl.ds(pl.multiple_of(b * BLOCK, BLOCK), BLOCK)], blank_sems.at[b]
            )

        if side_n:
            blank[...] = jnp.zeros_like(blank)
            each(sc[4], slots, lambda b: clear(b).start())

        @pl.when(recv == 1)
        def _():
            for k in range(len(jobs)):
                fetch(k).start()
            for k in range(len(jobs)):
                fetch(k).wait()
                store(k).start()
            for k in range(len(jobs)):
                store(k).wait()

        if side_n:
            count = jnp.minimum(c_n, side_n)
            each(0, count, lambda b: side_fetch(b).start())

            def pass_on(b):
                side_fetch(b).wait()
                side_store(b).start()

            each(0, count, pass_on)
            each(0, count, lambda b: side_store(b).wait())
            each(sc[4], slots, lambda b: clear(b).wait())

    any_spec = pl.BlockSpec(memory_space=pl.ANY)
    side_rows = max(side_n * BLOCK, UNIT)
    return pl.pallas_call(
        kernel,
        grid_spec=pltpu.PrefetchScalarGridSpec(
            num_scalar_prefetch=1,
            grid=(),
            in_specs=[any_spec] * (len(operands) + 1),
            out_specs=any_spec,
            scratch_shapes=[
                pltpu.VMEM((staged, features), out_w.dtype),
                pltpu.VMEM((side_rows, features), out_w.dtype),
                pltpu.SemaphoreType.DMA((2 * len(jobs),)),
                pltpu.SemaphoreType.DMA((2 * max(side_n, 1),)),
                pltpu.VMEM((BLOCK if side_n else UNIT, features), out_w.dtype),
                pltpu.SemaphoreType.DMA((slots,)),
            ],
        ),
        out_shape=jax.ShapeDtypeStruct(out_w.shape, out_w.dtype),
        input_output_aliases={len(operands) + 1: 0},
        compiler_params=pltpu.CompilerParams(
            vmem_limit_bytes=(staged + side_rows + BLOCK) * features * 2 + (2 << 20)
        ),
        cost_estimate=HINT,
        name="place_rows",
    )(scalars, *operands, out_w)


def place_states(scalars, slots, own, side, across, latent_rows):
    rows = own.shape[0]
    seqs = (rows - latent_rows) // 4

    def kernel(sc, own_ref, side_ref, across_ref, ssm, conv, turned):
        own_src, own_n, own_dst, filled = sc[1], sc[2], sc[3], sc[4]
        recv, recv_dst = sc[5], sc[6] // BLOCK
        c_src, c_n, c_dst = sc[8], sc[9], sc[10]

        def rows_of(b):
            return pl.ds(pl.multiple_of(b * BLOCK, BLOCK), BLOCK)

        def put(b, ref, at):
            block = ref[:, rows_of(at)].astype(F32)
            ssm[rows_of(b), :] = block[:latent_rows].T
            for k in range(4):
                at = latent_rows + k * seqs
                turned[pl.ds(k, seqs, stride=4), :] = block[at : at + seqs]
            conv[:, rows_of(b)] = turned[...]

        across_n = across_ref.shape[1] // BLOCK

        def empty(b):
            ssm[rows_of(b), :] = jnp.zeros((BLOCK, latent_rows), F32)
            conv[:, rows_of(b)] = jnp.zeros((rows - latent_rows, BLOCK), F32)

        first = jnp.where(recv == 1, recv_dst, 0)
        count = jnp.where(recv == 1, across_n, 0)
        each(own_dst, own_dst + own_n, lambda b: put(b, own_ref, b - own_dst + own_src))
        each(c_dst, c_dst + c_n, lambda b: put(b, side_ref, b - c_dst + c_src))
        each(first, first + count, lambda b: put(b, across_ref, b - recv_dst))
        each(filled, slots, empty)

    vmem = pl.BlockSpec(memory_space=pltpu.VMEM)
    return pl.pallas_call(
        kernel,
        grid_spec=pltpu.PrefetchScalarGridSpec(
            num_scalar_prefetch=1,
            grid=(),
            in_specs=[vmem] * 3,
            out_specs=[vmem] * 2,
            scratch_shapes=[pltpu.VMEM((rows - latent_rows, BLOCK), F32)],
        ),
        out_shape=(
            jax.ShapeDtypeStruct((slots * BLOCK, latent_rows), F32),
            jax.ShapeDtypeStruct((rows - latent_rows, slots * BLOCK), F32),
        ),
        compiler_params=pltpu.CompilerParams(vmem_limit_bytes=24 << 20),
        cost_estimate=HINT,
        name="place_states",
    )(scalars, own, side, across)


def split(blocks):
    return blocks, (blocks + 1) // 3


def neighbours(x, z, dt, enter, leave, w, ssm, conv, logs, taps, offs, inc, res, ranks, tallies):
    groups, depth = lax.axis_size("groups"), lax.axis_size("dp")
    old_blocks = w.shape[0] // BLOCK
    cap = (logs.shape[0] // BLOCK) // 3 + 2
    most = cap - old_blocks
    half = 2 * old_blocks
    fewest = half - cap

    def place(a, b, c):
        return (a * 4 + b) * depth + c

    every = [(a, c) for a in range(groups) for c in range(depth)]
    across = [(place(a, u, c), place(a, 3 - u, c)) for a, c in every for u in (1, 2)]
    along_x = [(place(a, u, c), place(1 - a, u, c)) for a, c in every for u in (1, 2)]
    along_z = [(place(a, u, c), place(a, u, c ^ 1)) for a, c in every for u in (1, 2)]
    inside = [(place(a, u, c), place(a, v, c)) for a, c in every for u, v in ((1, 0), (2, 3))]
    cores = [(place(a, u, c), place(a, u ^ 1, c)) for a, c in every for u in range(4)]
    chips = [(place(a, u, c), place(a, u ^ 2, c)) for a, c in every for u in range(4)]

    def plan(ranks, tallies, pick, scalars, lane0, lane1):
        g, t, d = (lax.axis_index(a) for a in AXES)
        q = 2 * g + (d & 1)
        middle, t0, t1, t2 = ranks[1], tallies[0], tallies[1], tallies[2]
        is_mid = (t == middle).astype(jnp.int32)
        crossing = jnp.where(middle == 2, half - t0, half - t2)
        def by_rank(first, low, high, last):
            return jnp.where(t == 0, first, jnp.where(t == 3, last, jnp.where(t == 1, low, high)))

        pick[0] = jnp.clip(crossing - fewest, 0, old_blocks - 2 - fewest)
        base = jnp.where(t == 1, (old_blocks - crossing) * BLOCK, 0)
        early, relay = split(crossing)
        lane0[0] = base
        lane1[0] = by_rank(0, 0, (old_blocks - most) * BLOCK, 0)

        values = [
            t,
            0,
            by_rank(old_blocks, is_mid * (half - t0), is_mid * (half - t2), old_blocks),
            by_rank(0, 0, crossing, t2 - old_blocks),
            by_rank(t0, is_mid * t1, is_mid * t1, t2),
            is_mid,
            by_rank(0, (half - t0) * BLOCK, 0, 0),
            q,
            by_rank(0, 0, 0, most - (t2 - old_blocks)),
            by_rank(t0 - old_blocks, 0, 0, t2 - old_blocks),
            by_rank(old_blocks, 0, 0, 0),
            by_rank(2 * old_blocks, 0, old_blocks - most, 2 * old_blocks),
            base + 2 * crossing * q * UNIT,
            base + (2 * crossing * q + early) * UNIT,
            base + (2 * crossing * (3 - q) + 2 * relay) * UNIT,
        ]
        values[1] = by_rank(0, is_mid * (t0 - old_blocks), 0, 0)
        for k, value in enumerate(values):
            scalars[k] = value

    smem = pl.BlockSpec(memory_space=pltpu.SMEM)
    one = jax.ShapeDtypeStruct((1,), jnp.int32)
    pick, scalars, lane0, lane1 = pl.pallas_call(
        plan,
        in_specs=[smem] * 2,
        out_specs=[smem] * 4,
        out_shape=(one, jax.ShapeDtypeStruct((15,), jnp.int32)) + (one,) * 2,
        name="plan",
    )(ranks, tallies)
    pick, lane0, lane1 = (a.reshape(()) for a in (pick, lane0, lane1))

    def permute(a, pairs):
        return lax.ppermute(a, AXES, pairs)

    tie = lax.optimization_barrier

    def body(v, args):
        scalars, lane0, lane1, x, z, dt, enter, leave, w, ssm, conv, *params = args
        early, relay = split(v)
        late = 2 * v - early
        n, k, m = early * UNIT, late * UNIT, relay * UNIT
        far_n = n + k - 2 * m

        first = cut_rows(scalars, w, n)
        y1 = permute(first, across)
        scalars, first = tie((scalars, first))
        out_w, side, second, third, partial, states = decode_here(
            scalars, cap, most, (k, far_n), x, z, dt, enter, leave, w, ssm, conv, *params
        )
        to_across = lax.dynamic_slice_in_dim(states, lane0, v * BLOCK, 1)
        second, to_across = tie((second, to_across))
        across_s = permute(to_across, across)
        y2 = permute(second, across)
        y1, states, partial, side = tie((y1, states, partial, side))
        x1, z1 = permute(y1, along_x), permute(y1, along_z)

        features = partial.shape[1]
        odd = scalars[0] & 1
        core = odd * (features // 2)
        mine = lax.dynamic_slice_in_dim(partial, core, features // 2, 1)
        theirs = lax.dynamic_slice_in_dim(partial, features // 2 - core, features // 2, 1)
        chip_sum = (mine + permute(theirs, cores)).astype(BF)
        total = (chip_sum.astype(F32) + permute(chip_sum, chips).astype(F32)).astype(BF)
        side_s = permute(lax.dynamic_slice_in_dim(states, lane1, most * BLOCK, 1), inside)

        third, _, total, across_s = tie((third, y2, total, across_s))
        y3 = permute(third, across)
        x2, z2 = permute(y2, along_x), permute(y2, along_z)
        side = permute(side, inside)
        x1, z1, side = tie((x1, z1, side))
        to_x, to_z = z1[:m], x1[m : 2 * m]
        x3, z3 = permute(to_x, along_x), permute(to_z, along_z)
        scalars, to_x, to_z = tie((scalars, to_x, to_z))
        other = permute(total, cores)
        decoded = jnp.concatenate(
            [jnp.where(odd == 0, total, other), jnp.where(odd == 0, other, total)], axis=1
        )
        out_w = place_rows(
            scalars,
            out_w,
            [
                (y1, 0, n, lambda q: 2 * v * q),
                (y2, 0, k, lambda q: 2 * v * q + early),
                (x1, 0, n, lambda q: 2 * v * (q ^ 2)),
                (z1, 0, n, lambda q: 2 * v * (q ^ 1)),
            ],
            side,
        )
        new_ssm, new_conv = place_states(scalars, cap, states, side_s, across_s, ssm.shape[1])
        out_w = place_rows(
            scalars,
            out_w,
            [
                (x2, 0, k, lambda q: 2 * v * (q ^ 2) + early),
                (z2, 0, k, lambda q: 2 * v * (q ^ 1) + early),
                (x3, 0, m, lambda q: 2 * v * (3 - q)),
                (z3, 0, m, lambda q: 2 * v * (3 - q) + relay),
                (y3, 0, far_n, lambda q: 2 * v * (3 - q) + 2 * relay),
            ],
        )
        return decoded, out_w, new_ssm, new_conv

    args = (scalars, lane0, lane1, x, z, dt, enter, leave, w, ssm, conv, logs, taps, offs, inc, res)
    branches = [lambda args, v=v: body(v, args) for v in range(fewest, old_blocks - 1)]
    decoded, out_w, new_ssm, new_conv = lax.switch(pick, branches, args)
    return decoded.reshape(x.shape[0], x.shape[1], -1), out_w, new_ssm, new_conv.T


def solution(mesh):
    placed = (
        P(None, ("groups", "dp"), "tp"),
        P(None, ("groups", "dp"), "tp"),
        P(None, ("groups", "dp"), "tp"),
        P(None, ("groups", "dp"), None),
        P(None, ("groups", "dp"), None),
        P("tp", None),
        P("tp", ("groups", "dp")),
        P("tp", ("groups", "dp")),
    ) + (P(),) * 7
    square = mesh.shape["tp"] == 4 and mesh.shape["groups"] == 2 and mesh.shape["dp"] % 2 == 0
    return jax.shard_map(
        neighbours if square else general,
        mesh=mesh,
        in_specs=placed,
        out_specs=(
            P(None, ("groups", "dp"), None),
            P(("groups", "tp"), None),
            P("tp", ("groups", "dp")),
            P("tp", ("groups", "dp")),
        ),
        check_vma=False,
    )
```

```python
import jax
import jax.numpy as jnp
from jax import lax
from jax.experimental import pallas as pl
from jax.experimental.pallas import tpu as pltpu
from jax.sharding import PartitionSpec as P

BLOCK = 128
UNIT = 16
BF = jnp.bfloat16
F32 = jnp.float32
AXES = ("groups", "tp", "dp")


def owner_ranges(remaining_ranks, holder_segment_tallies, holder_ranks):
    starts = jnp.cumsum(holder_segment_tallies) - holder_segment_tallies
    roster = jnp.arange(holder_ranks, dtype=jnp.int32)
    match = (remaining_ranks[None, :] == roster[:, None]).astype(jnp.int32)
    first = jnp.sum(match * starts[None, :], axis=1)
    total = jnp.sum(match * holder_segment_tallies[None, :], axis=1)
    return first, total


def pack_rows(columns, first, total, slot_rows):
    padded = jnp.pad(columns, ((0, slot_rows), (0, 0)))
    places = jnp.arange(slot_rows, dtype=jnp.int32)

    def one_owner(start, count):
        rows = lax.dynamic_slice_in_dim(padded, start * BLOCK, slot_rows, 0)
        return jnp.where((places < count * BLOCK)[:, None], rows, jnp.zeros_like(rows))

    packed = jax.vmap(one_owner)(first, total)
    return packed.reshape(-1, columns.shape[1])


def relocate_everywhere(rows, first, total, slot_rows):
    spread = lax.all_to_all(rows, "tp", split_axis=1, concat_axis=0, tiled=True)
    packed = pack_rows(spread, first, total, slot_rows)
    return lax.all_to_all(packed, "tp", split_axis=0, concat_axis=1, tiled=True)


def decode_plain(x, z, dt, enter, leave, ssm, conv, logs, taps, offs, inc, res, weights):
    steps, seqs, channels = x.shape
    h = ssm.reshape(channels, seqs, -1)
    window = conv.reshape(channels, seqs, 4)
    decay = -jnp.exp(logs)
    gated = []
    for step in range(steps):
        now = x[step].astype(F32).T
        window = jnp.concatenate([window[:, :, 1:], now[:, :, None]], axis=2)
        inner = jax.nn.silu(jnp.sum(window * taps[:, None, :], axis=2) + offs[:, None])
        delta = jax.nn.softplus(dt[step].astype(F32).T + inc[:, None])
        h = (
            jnp.exp(delta[:, :, None] * decay[:, None, :]) * h
            + (delta * inner)[:, :, None] * enter[step][None, :, :]
        )
        y = jnp.sum(h * leave[step][None, :, :], axis=2) + res[:, None] * inner
        gated.append((y * jax.nn.silu(z[step].astype(F32).T)).astype(BF))
    gated = jnp.concatenate(gated, axis=1)
    partial = lax.dot_general(
        gated, weights, (((0,), (0,)), ((), ())), preferred_element_type=F32
    )
    return partial, h.reshape(channels, -1), window.reshape(channels, -1)


def general(x, z, dt, enter, leave, w, ssm, conv, logs, taps, offs, inc, res, ranks, tallies):
    holders = lax.axis_size("tp")
    mine = lax.axis_index("tp")
    width, old = logs.shape[0], w.shape[0]
    slot_rows = (width // BLOCK // (holders * 3 // 4) + 2) * BLOCK
    first, total = owner_ranges(ranks, tallies, holders)

    def own(a):
        return lax.dynamic_slice_in_dim(a, mine * old, old, 0)

    moved_w = relocate_everywhere(w, first, total, slot_rows)
    partial, ssm, conv = decode_plain(
        x, z, dt, enter, leave, ssm, conv, own(logs), own(taps), own(offs), own(inc), own(res), w
    )
    decoded = lax.psum(partial, "tp").astype(BF).reshape(x.shape[0], x.shape[1], -1)
    return (
        decoded,
        moved_w,
        relocate_everywhere(ssm, first, total, slot_rows),
        relocate_everywhere(conv, first, total, slot_rows),
    )


def each(low, high, act):
    lax.fori_loop(low, high, lambda b, _: (act(b), 0)[1], 0)


CHUNK = 256
WIDE = 2048


def decode_kernel(
    sc, x, z, dt, enter, leave, h0, hist, logs, taps, offs, inc, res, w_all,
    out_w, side, second, third, partial, states, ys, deltas, feeds, turned, w, w_sem, own_sem, side_sem, cut_sem,
):
    i = pl.program_id(0)
    steps, seqs, chunk = x.shape
    latents = logs.shape[0]
    per = chunk // BLOCK
    blocks = w_all.shape[0] // BLOCK
    slots = out_w.shape[0] // BLOCK
    side_n = side.shape[0] // BLOCK
    own_src, own_n, own_dst, side_src = sc[1], sc[2], sc[3], sc[11]

    def rows(b):
        return pl.ds(pl.multiple_of(b * BLOCK, BLOCK), BLOCK)

    def fetch(b):
        return pltpu.make_async_copy(w_all.at[rows(b)], w.at[rows(b)], w_sem.at[b])

    def keep(b):
        at = jnp.clip(b - own_src + own_dst, 0, slots - 1)
        return pltpu.make_async_copy(w.at[rows(b)], out_w.at[rows(at)], own_sem.at[b])

    def pass_on(b):
        at = jnp.clip(b - side_src, 0, side_n - 1)
        return pltpu.make_async_copy(w.at[rows(b)], side.at[rows(at)], side_sem.at[b])

    @pl.when(i == 0)
    def _():
        each(0, blocks, lambda b: fetch(b).start())
        partial[...] = jnp.zeros_like(partial)

    decay = -jnp.exp(logs[...])
    xs = [x[t].astype(F32) for t in range(steps)]
    window = [hist[k] for k in range(1, 4)] + xs
    tap = [taps[k : k + 1, :] for k in range(4)]
    inners = []
    for t in range(steps):
        mixed = offs[...] + sum(window[t + k] * tap[k] for k in range(4))
        inner = mixed / (1.0 + jnp.exp(-mixed))
        v = dt[t].astype(F32) + inc[...]
        delta = jnp.maximum(v, 0.0) + jnp.log1p(jnp.exp(-jnp.abs(v)))
        inners.append(inner)
        deltas[t * seqs : (t + 1) * seqs, :] = delta
        feeds[t * seqs : (t + 1) * seqs, :] = delta * inner
    turned[...] = h0[...].T

    def wide(a):
        return jnp.concatenate([a] * per, axis=1)

    def sequence(s, _):
        at = pl.ds(pl.multiple_of(s * latents, latents), latents)
        h = turned[at, :]
        for t in range(steps):
            c = t * seqs + s
            row = pl.ds(c, 1)
            h = jnp.exp(deltas[row, :] * decay) * h + feeds[row, :] * wide(enter[c])
            ys[row, :] = jnp.sum(h * wide(leave[c]), axis=0, keepdims=True)
        states[at, :] = h.astype(BF)
        return 0

    lax.fori_loop(0, seqs, sequence, 0)
    states[seqs * latents :, :] = jnp.concatenate(xs, axis=0).astype(BF)
    gated = []
    for t in range(steps):
        y = ys[t * seqs : (t + 1) * seqs, :] + res[...] * inners[t]
        g = z[t].astype(F32)
        gated.append(y * (g / (1.0 + jnp.exp(-g))))
    gated = jnp.concatenate(gated, axis=0).astype(BF)

    def arrived(j, _):
        b = i * per + j
        fetch(b).wait()

        @pl.when((b >= own_src) & (b < own_src + own_n))
        def _():
            keep(b).start()

        @pl.when((b >= side_src) & (b < side_src + side_n))
        def _():
            pass_on(b).start()

        return 0

    lax.fori_loop(0, per, arrived, 0)
    last = i == pl.num_programs(0) - 1
    cuts = [
        pltpu.make_async_copy(
            w.at[pl.ds(pl.multiple_of(sc[row], UNIT), to.shape[0])], to, cut_sem.at[k]
        )
        for k, (row, to) in enumerate(((13, second), (14, third)))
    ]

    @pl.when(last)
    def _():
        for copy in cuts:
            copy.start()

    here = pl.ds(pl.multiple_of(i * chunk, chunk), chunk)

    def project(k):
        cols = pl.ds(pl.multiple_of(k * WIDE, WIDE), WIDE)
        partial[:, cols] += jnp.dot(gated, w[here, cols], preferred_element_type=F32)

    each(0, partial.shape[1] // WIDE, project)

    @pl.when(last)
    def _():
        for copy in cuts:
            copy.wait()
        each(own_src, own_src + own_n, lambda b: keep(b).wait())
        each(side_src, jnp.minimum(side_src + side_n, blocks), lambda b: pass_on(b).wait())


def decode_here(scalars, slots, side_n, cut_rows, x, z, dt, enter, leave, w, ssm, conv, logs, taps, offs, inc, res):
    steps, seqs, channels = x.shape
    latents = logs.shape[1]
    features = w.shape[1]
    n = channels // CHUNK
    series = pl.BlockSpec((steps, seqs, CHUNK), lambda i, sc: (0, 0, i))
    small = pl.BlockSpec((steps * seqs, latents, BLOCK), lambda i, sc: (0, 0, 0))

    def lanes(rows):
        return pl.BlockSpec((rows, CHUNK), lambda i, sc: (0, sc[0] * n + i))

    grid_spec = pltpu.PrefetchScalarGridSpec(
        num_scalar_prefetch=1,
        grid=(n,),
        in_specs=[
            series, series, series, small, small,
            pl.BlockSpec((CHUNK, seqs * latents), lambda i, sc: (i, 0)),
            pl.BlockSpec((4, seqs, CHUNK), lambda i, sc: (0, 0, i)),
            lanes(latents), lanes(4), lanes(1), lanes(1), lanes(1),
            pl.BlockSpec(memory_space=pltpu.HBM),
        ],
        out_specs=[
            pl.BlockSpec(memory_space=pltpu.HBM),
            pl.BlockSpec(memory_space=pltpu.HBM),
            pl.BlockSpec(memory_space=pltpu.HBM),
            pl.BlockSpec(memory_space=pltpu.HBM),
            pl.BlockSpec((steps * seqs, features), lambda i, sc: (0, 0)),
            pl.BlockSpec((seqs * (latents + 4), CHUNK), lambda i, sc: (0, i)),
        ],
        scratch_shapes=[
            pltpu.VMEM((steps * seqs, CHUNK), F32),
            pltpu.VMEM((steps * seqs, CHUNK), F32),
            pltpu.VMEM((steps * seqs, CHUNK), F32),
            pltpu.VMEM((seqs * latents, CHUNK), F32),
            pltpu.VMEM((channels, features), BF),
            pltpu.SemaphoreType.DMA((channels // BLOCK,)),
            pltpu.SemaphoreType.DMA((channels // BLOCK,)),
            pltpu.SemaphoreType.DMA((channels // BLOCK,)),
            pltpu.SemaphoreType.DMA((2,)),
        ],
    )
    rows = steps * seqs
    return pl.pallas_call(
        decode_kernel,
        grid_spec=grid_spec,
        out_shape=(
            jax.ShapeDtypeStruct((slots * BLOCK, features), BF),
            jax.ShapeDtypeStruct((side_n * BLOCK, features), BF),
            jax.ShapeDtypeStruct((cut_rows[0], features), BF),
            jax.ShapeDtypeStruct((cut_rows[1], features), BF),
            jax.ShapeDtypeStruct((rows, features), F32),
            jax.ShapeDtypeStruct((seqs * (latents + 4), channels), BF),
        ),
        compiler_params=pltpu.CompilerParams(vmem_limit_bytes=50 << 20),
        cost_estimate=HINT,
        name="decode",
    )(
        scalars, x, z, dt,
        jnp.broadcast_to(enter.reshape(rows, latents, 1), (rows, latents, BLOCK)),
        jnp.broadcast_to(leave.reshape(rows, latents, 1), (rows, latents, BLOCK)),
        ssm, conv.T.reshape(seqs, 4, channels).transpose(1, 0, 2), logs.T, taps.T,
        offs.reshape(1, -1), inc.reshape(1, -1), res.reshape(1, -1), w,
    )


HINT = pl.CostEstimate(flops=0, bytes_accessed=1024, transcendentals=0)


def cut_rows(scalars, w, rows):
    def kernel(sc, w_ref, out, sem):
        copy = pltpu.make_async_copy(
            w_ref.at[pl.ds(pl.multiple_of(sc[12], UNIT), rows)], out, sem
        )
        copy.start()
        copy.wait()

    return pl.pallas_call(
        kernel,
        grid_spec=pltpu.PrefetchScalarGridSpec(
            num_scalar_prefetch=1,
            grid=(),
            in_specs=[pl.BlockSpec(memory_space=pltpu.HBM)],
            out_specs=pl.BlockSpec(memory_space=pltpu.VMEM),
            scratch_shapes=[pltpu.SemaphoreType.DMA],
        ),
        out_shape=jax.ShapeDtypeStruct((rows, w.shape[1]), w.dtype),
        compiler_params=pltpu.CompilerParams(vmem_limit_bytes=8 << 20),
        cost_estimate=HINT,
        name="cut_rows",
    )(scalars, w)


def place_rows(scalars, out_w, pieces, side=None, blanks=False):
    slots, features = out_w.shape[0] // BLOCK, out_w.shape[1]
    arrays = []
    for piece in pieces:
        if not any(piece[0] is a for a in arrays):
            arrays.append(piece[0])
    jobs = []
    for array, first, rows, offset in pieces:
        jobs.append((next(k for k, a in enumerate(arrays) if a is array), first, rows, offset))
    side_n = 0 if side is None else side.shape[0] // BLOCK
    operands = arrays + ([] if side is None else [side])
    staged = sum(job[2] for job in jobs)

    def kernel(sc, *refs):
        ins, out = refs[: len(operands)], refs[len(operands) + 1]
        stage, side_stage, sems, side_sems, blank, blank_sems = refs[len(operands) + 2 :]
        recv, row0, q = sc[5], sc[6], sc[7]
        c_src, c_n, c_dst = sc[8], sc[9], sc[10]
        starts = [sum(job[2] for job in jobs[:k]) for k in range(len(jobs))]

        def fetch(k):
            which, first, rows, _ = jobs[k]
            return pltpu.make_async_copy(
                ins[which].at[pl.ds(first, rows)],
                stage.at[pl.ds(starts[k], rows)],
                sems.at[2 * k],
            )

        def store(k):
            _, _, rows, offset = jobs[k]
            row = jnp.clip(row0 + offset(q) * UNIT, 0, slots * BLOCK - rows)
            return pltpu.make_async_copy(
                stage.at[pl.ds(starts[k], rows)],
                out.at[pl.ds(pl.multiple_of(row, UNIT), rows)],
                sems.at[2 * k + 1],
            )

        def side_fetch(b):
            src = jnp.clip(c_src + b, 0, side_n - 1) * BLOCK
            return pltpu.make_async_copy(
                ins[-1].at[pl.ds(pl.multiple_of(src, BLOCK), BLOCK)],
                side_stage.at[pl.ds(pl.multiple_of(b * BLOCK, BLOCK), BLOCK)],
                side_sems.at[2 * b],
            )

        def side_store(b):
            dst = jnp.clip(c_dst + b, 0, slots - 1) * BLOCK
            return pltpu.make_async_copy(
                side_stage.at[pl.ds(pl.multiple_of(b * BLOCK, BLOCK), BLOCK)],
                out.at[pl.ds(pl.multiple_of(dst, BLOCK), BLOCK)],
                side_sems.at[2 * b + 1],
            )

        def clear(b):
            return pltpu.make_async_copy(
                blank, out.at[pl.ds(pl.multiple_of(b * BLOCK, BLOCK), BLOCK)], blank_sems.at[b]
            )

        if blanks:
            blank[...] = jnp.zeros_like(blank)
            each(sc[4], slots, lambda b: clear(b).start())

        @pl.when(recv == 1)
        def _():
            for k in range(len(jobs)):
                fetch(k).start()
            for k in range(len(jobs)):
                fetch(k).wait()
                store(k).start()
            for k in range(len(jobs)):
                store(k).wait()

        if side_n:
            count = jnp.minimum(c_n, side_n)
            each(0, count, lambda b: side_fetch(b).start())

            def pass_on(b):
                side_fetch(b).wait()
                side_store(b).start()

            each(0, count, pass_on)
            each(0, count, lambda b: side_store(b).wait())

        if blanks:
            each(sc[4], slots, lambda b: clear(b).wait())

    any_spec = pl.BlockSpec(memory_space=pl.ANY)
    side_rows = max(side_n * BLOCK, UNIT)
    return pl.pallas_call(
        kernel,
        grid_spec=pltpu.PrefetchScalarGridSpec(
            num_scalar_prefetch=1,
            grid=(),
            in_specs=[any_spec] * (len(operands) + 1),
            out_specs=any_spec,
            scratch_shapes=[
                pltpu.VMEM((staged, features), out_w.dtype),
                pltpu.VMEM((side_rows, features), out_w.dtype),
                pltpu.SemaphoreType.DMA((2 * len(jobs),)),
                pltpu.SemaphoreType.DMA((2 * max(side_n, 1),)),
                pltpu.VMEM((BLOCK if blanks else UNIT, features), out_w.dtype),
                pltpu.SemaphoreType.DMA((slots,)),
            ],
        ),
        out_shape=jax.ShapeDtypeStruct(out_w.shape, out_w.dtype),
        input_output_aliases={len(operands) + 1: 0},
        compiler_params=pltpu.CompilerParams(
            vmem_limit_bytes=(staged + side_rows + BLOCK) * features * 2 + (2 << 20)
        ),
        cost_estimate=HINT,
        name="place_rows",
    )(scalars, *operands, out_w)


def place_states(scalars, slots, own, side, across, latent_rows):
    rows = own.shape[0]
    seqs = (rows - latent_rows) // 4

    def kernel(sc, own_ref, side_ref, across_ref, ssm, conv, turned):
        own_src, own_n, own_dst, filled = sc[1], sc[2], sc[3], sc[4]
        recv, recv_dst = sc[5], sc[6] // BLOCK
        c_src, c_n, c_dst = sc[8], sc[9], sc[10]

        def rows_of(b):
            return pl.ds(pl.multiple_of(b * BLOCK, BLOCK), BLOCK)

        def put(b, ref, at):
            block = ref[:, rows_of(at)].astype(F32)
            ssm[rows_of(b), :] = block[:latent_rows].T
            for k in range(4):
                at = latent_rows + k * seqs
                turned[pl.ds(k, seqs, stride=4), :] = block[at : at + seqs]
            conv[:, rows_of(b)] = turned[...]

        across_n = across_ref.shape[1] // BLOCK

        def empty(b):
            ssm[rows_of(b), :] = jnp.zeros((BLOCK, latent_rows), F32)
            conv[:, rows_of(b)] = jnp.zeros((rows - latent_rows, BLOCK), F32)

        first = jnp.where(recv == 1, recv_dst, 0)
        count = jnp.where(recv == 1, across_n, 0)
        each(own_dst, own_dst + own_n, lambda b: put(b, own_ref, b - own_dst + own_src))
        each(c_dst, c_dst + c_n, lambda b: put(b, side_ref, b - c_dst + c_src))
        each(first, first + count, lambda b: put(b, across_ref, b - recv_dst))
        each(filled, slots, empty)

    vmem = pl.BlockSpec(memory_space=pltpu.VMEM)
    return pl.pallas_call(
        kernel,
        grid_spec=pltpu.PrefetchScalarGridSpec(
            num_scalar_prefetch=1,
            grid=(),
            in_specs=[vmem] * 3,
            out_specs=[vmem] * 2,
            scratch_shapes=[pltpu.VMEM((rows - latent_rows, BLOCK), F32)],
        ),
        out_shape=(
            jax.ShapeDtypeStruct((slots * BLOCK, latent_rows), F32),
            jax.ShapeDtypeStruct((rows - latent_rows, slots * BLOCK), F32),
        ),
        compiler_params=pltpu.CompilerParams(vmem_limit_bytes=24 << 20),
        cost_estimate=HINT,
        name="place_states",
    )(scalars, own, side, across)


def split(blocks):
    return blocks, (5 * blocks + 5) // 11


def neighbours(x, z, dt, enter, leave, w, ssm, conv, logs, taps, offs, inc, res, ranks, tallies):
    groups, depth = lax.axis_size("groups"), lax.axis_size("dp")
    old_blocks = w.shape[0] // BLOCK
    cap = (logs.shape[0] // BLOCK) // 3 + 2
    most = cap - old_blocks
    half = 2 * old_blocks
    fewest = half - cap

    def place(a, b, c):
        return (a * 4 + b) * depth + c

    every = [(a, c) for a in range(groups) for c in range(depth)]
    across = [(place(a, u, c), place(a, 3 - u, c)) for a, c in every for u in (1, 2)]
    along_x = [(place(a, u, c), place(1 - a, u, c)) for a, c in every for u in (1, 2)]
    along_z = [(place(a, u, c), place(a, u, c ^ 1)) for a, c in every for u in (1, 2)]
    inside = [(place(a, u, c), place(a, v, c)) for a, c in every for u, v in ((1, 0), (2, 3))]
    cores = [(place(a, u, c), place(a, u ^ 1, c)) for a, c in every for u in range(4)]
    chips = [(place(a, u, c), place(a, u ^ 2, c)) for a, c in every for u in range(4)]

    def plan(ranks, tallies, pick, scalars, lane0, lane1):
        g, t, d = (lax.axis_index(a) for a in AXES)
        q = 2 * g + (d & 1)
        middle, t0, t1, t2 = ranks[1], tallies[0], tallies[1], tallies[2]
        is_mid = (t == middle).astype(jnp.int32)
        crossing = jnp.where(middle == 2, half - t0, half - t2)
        def by_rank(first, low, high, last):
            return jnp.where(t == 0, first, jnp.where(t == 3, last, jnp.where(t == 1, low, high)))

        pick[0] = jnp.clip(crossing - fewest, 0, old_blocks - 2 - fewest)
        base = jnp.where(t == 1, (old_blocks - crossing) * BLOCK, 0)
        early, relay = split(crossing)
        lane0[0] = base
        lane1[0] = by_rank(0, 0, (old_blocks - most) * BLOCK, 0)

        values = [
            t,
            0,
            by_rank(old_blocks, is_mid * (half - t0), is_mid * (half - t2), old_blocks),
            by_rank(0, 0, crossing, t2 - old_blocks),
            by_rank(t0, is_mid * t1, is_mid * t1, t2),
            is_mid,
            by_rank(0, (half - t0) * BLOCK, 0, 0),
            q,
            by_rank(0, 0, 0, most - (t2 - old_blocks)),
            by_rank(t0 - old_blocks, 0, 0, t2 - old_blocks),
            by_rank(old_blocks, 0, 0, 0),
            by_rank(2 * old_blocks, 0, old_blocks - most, 2 * old_blocks),
            base + 2 * crossing * q * UNIT,
            base + (2 * crossing * q + early) * UNIT,
            base + (2 * crossing * (3 - q) + 2 * relay) * UNIT,
        ]
        values[1] = by_rank(0, is_mid * (t0 - old_blocks), 0, 0)
        for k, value in enumerate(values):
            scalars[k] = value

    smem = pl.BlockSpec(memory_space=pltpu.SMEM)
    one = jax.ShapeDtypeStruct((1,), jnp.int32)
    pick, scalars, lane0, lane1 = pl.pallas_call(
        plan,
        in_specs=[smem] * 2,
        out_specs=[smem] * 4,
        out_shape=(one, jax.ShapeDtypeStruct((15,), jnp.int32)) + (one,) * 2,
        name="plan",
    )(ranks, tallies)
    pick, lane0, lane1 = (a.reshape(()) for a in (pick, lane0, lane1))

    def permute(a, pairs):
        return lax.ppermute(a, AXES, pairs)

    tie = lax.optimization_barrier

    def body(v, args):
        scalars, lane0, lane1, x, z, dt, enter, leave, w, ssm, conv, *params = args
        early, relay = split(v)
        second_n = 2 * v - early
        n, k, m = early * UNIT, second_n * UNIT, relay * UNIT
        far_n = n + k - 2 * m

        first = cut_rows(scalars, w, n)
        y1 = permute(first, across)
        scalars, first = tie((scalars, first))
        out_w, side, second, third, partial, states = decode_here(
            scalars, cap, most, (k, far_n), x, z, dt, enter, leave, w, ssm, conv, *params
        )
        y2 = permute(second, across)
        y1, states, partial, side = tie((y1, states, partial, side))
        x1, z1 = permute(y1, along_x), permute(y1, along_z)

        features = partial.shape[1]
        odd = scalars[0] & 1
        core = odd * (features // 2)
        mine = lax.dynamic_slice_in_dim(partial, core, features // 2, 1)
        theirs = lax.dynamic_slice_in_dim(partial, features // 2 - core, features // 2, 1)
        chip_sum = (mine + permute(theirs, cores)).astype(BF)
        total = (chip_sum.astype(F32) + permute(chip_sum, chips).astype(F32)).astype(BF)
        across_s = permute(lax.dynamic_slice_in_dim(states, lane0, v * BLOCK, 1), across)
        side_s = permute(lax.dynamic_slice_in_dim(states, lane1, most * BLOCK, 1), inside)

        y2, x1, z1, side, third, total, across_s, side_s = tie(
            (y2, x1, z1, side, third, total, across_s, side_s)
        )

        y3 = permute(third, across)
        x2, z2 = permute(y2, along_x), permute(y2, along_z)
        side = permute(side, inside)
        to_x, to_z = z1[:m], x1[m : 2 * m]
        x3, z3 = permute(to_x, along_x), permute(to_z, along_z)
        scalars, to_x, to_z = tie((scalars, to_x, to_z))
        other = permute(total, cores)
        decoded = jnp.concatenate(
            [jnp.where(odd == 0, total, other), jnp.where(odd == 0, other, total)], axis=1
        )
        out_w = place_rows(
            scalars,
            out_w,
            [
                (y1, 0, n, lambda q: 2 * v * q),
                (y2, 0, k, lambda q: 2 * v * q + early),
                (x1, 0, n, lambda q: 2 * v * (q ^ 2)),
                (z1, 0, n, lambda q: 2 * v * (q ^ 1)),
            ],
            blanks=True,
        )
        new_ssm, new_conv = place_states(scalars, cap, states, side_s, across_s, ssm.shape[1])
        out_w = place_rows(
            scalars,
            out_w,
            [
                (x2, 0, k, lambda q: 2 * v * (q ^ 2) + early),
                (z2, 0, k, lambda q: 2 * v * (q ^ 1) + early),
            ],
            side,
        )
        out_w = place_rows(
            scalars,
            out_w,
            [
                (x3, 0, m, lambda q: 2 * v * (3 - q)),
                (z3, 0, m, lambda q: 2 * v * (3 - q) + relay),
                (y3, 0, far_n, lambda q: 2 * v * (3 - q) + 2 * relay),
            ],
        )
        return decoded, out_w, new_ssm, new_conv

    args = (scalars, lane0, lane1, x, z, dt, enter, leave, w, ssm, conv, logs, taps, offs, inc, res)
    branches = [lambda args, v=v: body(v, args) for v in range(fewest, old_blocks - 1)]
    decoded, out_w, new_ssm, new_conv = lax.switch(pick, branches, args)
    return decoded.reshape(x.shape[0], x.shape[1], -1), out_w, new_ssm, new_conv.T


def solution(mesh):
    placed = (
        P(None, ("groups", "dp"), "tp"),
        P(None, ("groups", "dp"), "tp"),
        P(None, ("groups", "dp"), "tp"),
        P(None, ("groups", "dp"), None),
        P(None, ("groups", "dp"), None),
        P("tp", None),
        P("tp", ("groups", "dp")),
        P("tp", ("groups", "dp")),
    ) + (P(),) * 7
    square = mesh.shape["tp"] == 4 and mesh.shape["groups"] == 2 and mesh.shape["dp"] % 2 == 0
    return jax.shard_map(
        neighbours if square else general,
        mesh=mesh,
        in_specs=placed,
        out_specs=(
            P(None, ("groups", "dp"), None),
            P(("groups", "tp"), None),
            P("tp", ("groups", "dp")),
            P("tp", ("groups", "dp")),
        ),
        check_vma=False,
    )
```

```python
import jax
import jax.numpy as jnp
from jax import lax
from jax.experimental import pallas as pl
from jax.experimental.pallas import tpu as pltpu
from jax.sharding import PartitionSpec as P

BLOCK = 128
UNIT = 16
BF = jnp.bfloat16
F32 = jnp.float32
AXES = ("groups", "tp", "dp")


def owner_ranges(remaining_ranks, holder_segment_tallies, holder_ranks):
    starts = jnp.cumsum(holder_segment_tallies) - holder_segment_tallies
    roster = jnp.arange(holder_ranks, dtype=jnp.int32)
    match = (remaining_ranks[None, :] == roster[:, None]).astype(jnp.int32)
    first = jnp.sum(match * starts[None, :], axis=1)
    total = jnp.sum(match * holder_segment_tallies[None, :], axis=1)
    return first, total


def pack_rows(columns, first, total, slot_rows):
    padded = jnp.pad(columns, ((0, slot_rows), (0, 0)))
    places = jnp.arange(slot_rows, dtype=jnp.int32)

    def one_owner(start, count):
        rows = lax.dynamic_slice_in_dim(padded, start * BLOCK, slot_rows, 0)
        return jnp.where((places < count * BLOCK)[:, None], rows, jnp.zeros_like(rows))

    packed = jax.vmap(one_owner)(first, total)
    return packed.reshape(-1, columns.shape[1])


def relocate_everywhere(rows, first, total, slot_rows):
    spread = lax.all_to_all(rows, "tp", split_axis=1, concat_axis=0, tiled=True)
    packed = pack_rows(spread, first, total, slot_rows)
    return lax.all_to_all(packed, "tp", split_axis=0, concat_axis=1, tiled=True)


def decode_plain(x, z, dt, enter, leave, ssm, conv, logs, taps, offs, inc, res, weights):
    steps, seqs, channels = x.shape
    h = ssm.reshape(channels, seqs, -1)
    window = conv.reshape(channels, seqs, 4)
    decay = -jnp.exp(logs)
    gated = []
    for step in range(steps):
        now = x[step].astype(F32).T
        window = jnp.concatenate([window[:, :, 1:], now[:, :, None]], axis=2)
        inner = jax.nn.silu(jnp.sum(window * taps[:, None, :], axis=2) + offs[:, None])
        delta = jax.nn.softplus(dt[step].astype(F32).T + inc[:, None])
        h = (
            jnp.exp(delta[:, :, None] * decay[:, None, :]) * h
            + (delta * inner)[:, :, None] * enter[step][None, :, :]
        )
        y = jnp.sum(h * leave[step][None, :, :], axis=2) + res[:, None] * inner
        gated.append((y * jax.nn.silu(z[step].astype(F32).T)).astype(BF))
    gated = jnp.concatenate(gated, axis=1)
    partial = lax.dot_general(
        gated, weights, (((0,), (0,)), ((), ())), preferred_element_type=F32
    )
    return partial, h.reshape(channels, -1), window.reshape(channels, -1)


def general(x, z, dt, enter, leave, w, ssm, conv, logs, taps, offs, inc, res, ranks, tallies):
    holders = lax.axis_size("tp")
    mine = lax.axis_index("tp")
    width, old = logs.shape[0], w.shape[0]
    slot_rows = (width // BLOCK // (holders * 3 // 4) + 2) * BLOCK
    first, total = owner_ranges(ranks, tallies, holders)

    def own(a):
        return lax.dynamic_slice_in_dim(a, mine * old, old, 0)

    moved_w = relocate_everywhere(w, first, total, slot_rows)
    partial, ssm, conv = decode_plain(
        x, z, dt, enter, leave, ssm, conv, own(logs), own(taps), own(offs), own(inc), own(res), w
    )
    decoded = lax.psum(partial, "tp").astype(BF).reshape(x.shape[0], x.shape[1], -1)
    return (
        decoded,
        moved_w,
        relocate_everywhere(ssm, first, total, slot_rows),
        relocate_everywhere(conv, first, total, slot_rows),
    )


def each(low, high, act):
    lax.fori_loop(low, high, lambda b, _: (act(b), 0)[1], 0)


CHUNK = 256
WIDE = 2048


def decode_kernel(
    sc, x, z, dt, enter, leave, h0, hist, logs, taps, offs, inc, res, w_all,
    out_w, side, second, third, partial, states, ys, deltas, feeds, turned, w, w_sem, own_sem, side_sem, cut_sem,
):
    i = pl.program_id(0)
    steps, seqs, chunk = x.shape
    latents = logs.shape[0]
    per = chunk // BLOCK
    blocks = w_all.shape[0] // BLOCK
    slots = out_w.shape[0] // BLOCK
    side_n = side.shape[0] // BLOCK
    own_src, own_n, own_dst, side_src = sc[1], sc[2], sc[3], sc[11]

    def rows(b):
        return pl.ds(pl.multiple_of(b * BLOCK, BLOCK), BLOCK)

    def fetch(b):
        return pltpu.make_async_copy(w_all.at[rows(b)], w.at[rows(b)], w_sem.at[b])

    def keep(b):
        at = jnp.clip(b - own_src + own_dst, 0, slots - 1)
        return pltpu.make_async_copy(w.at[rows(b)], out_w.at[rows(at)], own_sem.at[b])

    def pass_on(b):
        at = jnp.clip(b - side_src, 0, side_n - 1)
        return pltpu.make_async_copy(w.at[rows(b)], side.at[rows(at)], side_sem.at[b])

    @pl.when(i == 0)
    def _():
        each(0, blocks, lambda b: fetch(b).start())
        partial[...] = jnp.zeros_like(partial)

    decay = -jnp.exp(logs[...])
    xs = [x[t].astype(F32) for t in range(steps)]
    window = [hist[k] for k in range(1, 4)] + xs
    tap = [taps[k : k + 1, :] for k in range(4)]
    inners = []
    for t in range(steps):
        mixed = offs[...] + sum(window[t + k] * tap[k] for k in range(4))
        inner = mixed / (1.0 + jnp.exp(-mixed))
        v = dt[t].astype(F32) + inc[...]
        delta = jnp.maximum(v, 0.0) + jnp.log1p(jnp.exp(-jnp.abs(v)))
        inners.append(inner)
        deltas[t * seqs : (t + 1) * seqs, :] = delta
        feeds[t * seqs : (t + 1) * seqs, :] = delta * inner
    turned[...] = h0[...].T

    def wide(a):
        return jnp.concatenate([a] * per, axis=1)

    def sequence(s, _):
        at = pl.ds(pl.multiple_of(s * latents, latents), latents)
        h = turned[at, :]
        for t in range(steps):
            c = t * seqs + s
            row = pl.ds(c, 1)
            h = jnp.exp(deltas[row, :] * decay) * h + feeds[row, :] * wide(enter[c])
            ys[row, :] = jnp.sum(h * wide(leave[c]), axis=0, keepdims=True)
        states[at, :] = h.astype(BF)
        return 0

    lax.fori_loop(0, seqs, sequence, 0)
    states[seqs * latents :, :] = jnp.concatenate(xs, axis=0).astype(BF)
    gated = []
    for t in range(steps):
        y = ys[t * seqs : (t + 1) * seqs, :] + res[...] * inners[t]
        g = z[t].astype(F32)
        gated.append(y * (g / (1.0 + jnp.exp(-g))))
    gated = jnp.concatenate(gated, axis=0).astype(BF)

    def arrived(j, _):
        b = i * per + j
        fetch(b).wait()

        @pl.when((b >= own_src) & (b < own_src + own_n))
        def _():
            keep(b).start()

        @pl.when((b >= side_src) & (b < side_src + side_n))
        def _():
            pass_on(b).start()

        return 0

    lax.fori_loop(0, per, arrived, 0)
    last = i == pl.num_programs(0) - 1
    cuts = [
        pltpu.make_async_copy(
            w.at[pl.ds(pl.multiple_of(sc[row], UNIT), to.shape[0])], to, cut_sem.at[k]
        )
        for k, (row, to) in enumerate(((13, second), (14, third)))
    ]

    @pl.when(last)
    def _():
        for copy in cuts:
            copy.start()

    here = pl.ds(pl.multiple_of(i * chunk, chunk), chunk)

    def project(k):
        cols = pl.ds(pl.multiple_of(k * WIDE, WIDE), WIDE)
        partial[:, cols] += jnp.dot(gated, w[here, cols], preferred_element_type=F32)

    each(0, partial.shape[1] // WIDE, project)

    @pl.when(last)
    def _():
        for copy in cuts:
            copy.wait()
        each(own_src, own_src + own_n, lambda b: keep(b).wait())
        each(side_src, jnp.minimum(side_src + side_n, blocks), lambda b: pass_on(b).wait())


def decode_here(scalars, slots, side_n, cut_rows, x, z, dt, enter, leave, w, ssm, conv, logs, taps, offs, inc, res):
    steps, seqs, channels = x.shape
    latents = logs.shape[1]
    features = w.shape[1]
    n = channels // CHUNK
    series = pl.BlockSpec((steps, seqs, CHUNK), lambda i, sc: (0, 0, i))
    small = pl.BlockSpec((steps * seqs, latents, BLOCK), lambda i, sc: (0, 0, 0))

    def lanes(rows):
        return pl.BlockSpec((rows, CHUNK), lambda i, sc: (0, sc[0] * n + i))

    grid_spec = pltpu.PrefetchScalarGridSpec(
        num_scalar_prefetch=1,
        grid=(n,),
        in_specs=[
            series, series, series, small, small,
            pl.BlockSpec((CHUNK, seqs * latents), lambda i, sc: (i, 0)),
            pl.BlockSpec((4, seqs, CHUNK), lambda i, sc: (0, 0, i)),
            lanes(latents), lanes(4), lanes(1), lanes(1), lanes(1),
            pl.BlockSpec(memory_space=pltpu.HBM),
        ],
        out_specs=[
            pl.BlockSpec(memory_space=pltpu.HBM),
            pl.BlockSpec(memory_space=pltpu.HBM),
            pl.BlockSpec(memory_space=pltpu.HBM),
            pl.BlockSpec(memory_space=pltpu.HBM),
            pl.BlockSpec((steps * seqs, features), lambda i, sc: (0, 0)),
            pl.BlockSpec((seqs * (latents + 4), CHUNK), lambda i, sc: (0, i)),
        ],
        scratch_shapes=[
            pltpu.VMEM((steps * seqs, CHUNK), F32),
            pltpu.VMEM((steps * seqs, CHUNK), F32),
            pltpu.VMEM((steps * seqs, CHUNK), F32),
            pltpu.VMEM((seqs * latents, CHUNK), F32),
            pltpu.VMEM((channels, features), BF),
            pltpu.SemaphoreType.DMA((channels // BLOCK,)),
            pltpu.SemaphoreType.DMA((channels // BLOCK,)),
            pltpu.SemaphoreType.DMA((channels // BLOCK,)),
            pltpu.SemaphoreType.DMA((2,)),
        ],
    )
    rows = steps * seqs
    return pl.pallas_call(
        decode_kernel,
        grid_spec=grid_spec,
        out_shape=(
            jax.ShapeDtypeStruct((slots * BLOCK, features), BF),
            jax.ShapeDtypeStruct((side_n * BLOCK, features), BF),
            jax.ShapeDtypeStruct((cut_rows[0], features), BF),
            jax.ShapeDtypeStruct((cut_rows[1], features), BF),
            jax.ShapeDtypeStruct((rows, features), F32),
            jax.ShapeDtypeStruct((seqs * (latents + 4), channels), BF),
        ),
        compiler_params=pltpu.CompilerParams(vmem_limit_bytes=50 << 20),
        cost_estimate=HINT,
        name="decode",
    )(
        scalars, x, z, dt,
        jnp.broadcast_to(enter.reshape(rows, latents, 1), (rows, latents, BLOCK)),
        jnp.broadcast_to(leave.reshape(rows, latents, 1), (rows, latents, BLOCK)),
        ssm, conv.T.reshape(seqs, 4, channels).transpose(1, 0, 2), logs.T, taps.T,
        offs.reshape(1, -1), inc.reshape(1, -1), res.reshape(1, -1), w,
    )


HINT = pl.CostEstimate(flops=0, bytes_accessed=1024, transcendentals=0)


def cut_rows(scalars, w, rows):
    def kernel(sc, w_ref, out, sem):
        copy = pltpu.make_async_copy(
            w_ref.at[pl.ds(pl.multiple_of(sc[12], UNIT), rows)], out, sem
        )
        copy.start()
        copy.wait()

    return pl.pallas_call(
        kernel,
        grid_spec=pltpu.PrefetchScalarGridSpec(
            num_scalar_prefetch=1,
            grid=(),
            in_specs=[pl.BlockSpec(memory_space=pltpu.HBM)],
            out_specs=pl.BlockSpec(memory_space=pltpu.VMEM),
            scratch_shapes=[pltpu.SemaphoreType.DMA],
        ),
        out_shape=jax.ShapeDtypeStruct((rows, w.shape[1]), w.dtype),
        compiler_params=pltpu.CompilerParams(vmem_limit_bytes=8 << 20),
        cost_estimate=HINT,
        name="cut_rows",
    )(scalars, w)


def place_rows(scalars, out_w, pieces, side=None, blanks=False):
    slots, features = out_w.shape[0] // BLOCK, out_w.shape[1]
    arrays = []
    for piece in pieces:
        if not any(piece[0] is a for a in arrays):
            arrays.append(piece[0])
    jobs = []
    for array, first, rows, offset in pieces:
        jobs.append((next(k for k, a in enumerate(arrays) if a is array), first, rows, offset))
    side_n = 0 if side is None else side.shape[0] // BLOCK
    operands = arrays + ([] if side is None else [side])
    staged = sum(job[2] for job in jobs)

    def kernel(sc, *refs):
        ins, out = refs[: len(operands)], refs[len(operands) + 1]
        stage, side_stage, sems, side_sems, blank, blank_sems = refs[len(operands) + 2 :]
        recv, row0, q = sc[5], sc[6], sc[7]
        c_src, c_n, c_dst = sc[8], sc[9], sc[10]
        starts = [sum(job[2] for job in jobs[:k]) for k in range(len(jobs))]

        def fetch(k):
            which, first, rows, _ = jobs[k]
            return pltpu.make_async_copy(
                ins[which].at[pl.ds(first, rows)],
                stage.at[pl.ds(starts[k], rows)],
                sems.at[2 * k],
            )

        def store(k):
            _, _, rows, offset = jobs[k]
            row = jnp.clip(row0 + offset(q) * UNIT, 0, slots * BLOCK - rows)
            return pltpu.make_async_copy(
                stage.at[pl.ds(starts[k], rows)],
                out.at[pl.ds(pl.multiple_of(row, UNIT), rows)],
                sems.at[2 * k + 1],
            )

        def side_fetch(b):
            src = jnp.clip(c_src + b, 0, side_n - 1) * BLOCK
            return pltpu.make_async_copy(
                ins[-1].at[pl.ds(pl.multiple_of(src, BLOCK), BLOCK)],
                side_stage.at[pl.ds(pl.multiple_of(b * BLOCK, BLOCK), BLOCK)],
                side_sems.at[2 * b],
            )

        def side_store(b):
            dst = jnp.clip(c_dst + b, 0, slots - 1) * BLOCK
            return pltpu.make_async_copy(
                side_stage.at[pl.ds(pl.multiple_of(b * BLOCK, BLOCK), BLOCK)],
                out.at[pl.ds(pl.multiple_of(dst, BLOCK), BLOCK)],
                side_sems.at[2 * b + 1],
            )

        def clear(b):
            return pltpu.make_async_copy(
                blank, out.at[pl.ds(pl.multiple_of(b * BLOCK, BLOCK), BLOCK)], blank_sems.at[b]
            )

        if blanks:
            blank[...] = jnp.zeros_like(blank)
            each(sc[4], slots, lambda b: clear(b).start())

        @pl.when(recv == 1)
        def _():
            for k in range(len(jobs)):
                fetch(k).start()
            for k in range(len(jobs)):
                fetch(k).wait()
                store(k).start()
            for k in range(len(jobs)):
                store(k).wait()

        if side_n:
            count = jnp.minimum(c_n, side_n)
            each(0, count, lambda b: side_fetch(b).start())

            def pass_on(b):
                side_fetch(b).wait()
                side_store(b).start()

            each(0, count, pass_on)
            each(0, count, lambda b: side_store(b).wait())

        if blanks:
            each(sc[4], slots, lambda b: clear(b).wait())

    any_spec = pl.BlockSpec(memory_space=pl.ANY)
    side_rows = max(side_n * BLOCK, UNIT)
    return pl.pallas_call(
        kernel,
        grid_spec=pltpu.PrefetchScalarGridSpec(
            num_scalar_prefetch=1,
            grid=(),
            in_specs=[any_spec] * (len(operands) + 1),
            out_specs=any_spec,
            scratch_shapes=[
                pltpu.VMEM((staged, features), out_w.dtype),
                pltpu.VMEM((side_rows, features), out_w.dtype),
                pltpu.SemaphoreType.DMA((2 * len(jobs),)),
                pltpu.SemaphoreType.DMA((2 * max(side_n, 1),)),
                pltpu.VMEM((BLOCK if blanks else UNIT, features), out_w.dtype),
                pltpu.SemaphoreType.DMA((slots,)),
            ],
        ),
        out_shape=jax.ShapeDtypeStruct(out_w.shape, out_w.dtype),
        input_output_aliases={len(operands) + 1: 0},
        compiler_params=pltpu.CompilerParams(
            vmem_limit_bytes=(staged + side_rows + BLOCK) * features * 2 + (2 << 20)
        ),
        cost_estimate=HINT,
        name="place_rows",
    )(scalars, *operands, out_w)


def place_states(scalars, slots, own, side, across, latent_rows):
    rows = own.shape[0]
    seqs = (rows - latent_rows) // 4

    def kernel(sc, own_ref, side_ref, across_ref, ssm, conv, turned):
        own_src, own_n, own_dst, filled = sc[1], sc[2], sc[3], sc[4]
        recv, recv_dst = sc[5], sc[6] // BLOCK
        c_src, c_n, c_dst = sc[8], sc[9], sc[10]

        def rows_of(b):
            return pl.ds(pl.multiple_of(b * BLOCK, BLOCK), BLOCK)

        def put(b, ref, at):
            block = ref[:, rows_of(at)].astype(F32)
            ssm[rows_of(b), :] = block[:latent_rows].T
            for k in range(4):
                at = latent_rows + k * seqs
                turned[pl.ds(k, seqs, stride=4), :] = block[at : at + seqs]
            conv[:, rows_of(b)] = turned[...]

        across_n = across_ref.shape[1] // BLOCK

        def empty(b):
            ssm[rows_of(b), :] = jnp.zeros((BLOCK, latent_rows), F32)
            conv[:, rows_of(b)] = jnp.zeros((rows - latent_rows, BLOCK), F32)

        first = jnp.where(recv == 1, recv_dst, 0)
        count = jnp.where(recv == 1, across_n, 0)
        each(own_dst, own_dst + own_n, lambda b: put(b, own_ref, b - own_dst + own_src))
        each(c_dst, c_dst + c_n, lambda b: put(b, side_ref, b - c_dst + c_src))
        each(first, first + count, lambda b: put(b, across_ref, b - recv_dst))
        each(filled, slots, empty)

    vmem = pl.BlockSpec(memory_space=pltpu.VMEM)
    return pl.pallas_call(
        kernel,
        grid_spec=pltpu.PrefetchScalarGridSpec(
            num_scalar_prefetch=1,
            grid=(),
            in_specs=[vmem] * 3,
            out_specs=[vmem] * 2,
            scratch_shapes=[pltpu.VMEM((rows - latent_rows, BLOCK), F32)],
        ),
        out_shape=(
            jax.ShapeDtypeStruct((slots * BLOCK, latent_rows), F32),
            jax.ShapeDtypeStruct((rows - latent_rows, slots * BLOCK), F32),
        ),
        compiler_params=pltpu.CompilerParams(vmem_limit_bytes=24 << 20),
        cost_estimate=HINT,
        name="place_states",
    )(scalars, own, side, across)


def split(blocks):
    return blocks, (3 * blocks + 5) // 11


def neighbours(x, z, dt, enter, leave, w, ssm, conv, logs, taps, offs, inc, res, ranks, tallies):
    groups, depth = lax.axis_size("groups"), lax.axis_size("dp")
    old_blocks = w.shape[0] // BLOCK
    cap = (logs.shape[0] // BLOCK) // 3 + 2
    most = cap - old_blocks
    half = 2 * old_blocks
    fewest = half - cap

    def place(a, b, c):
        return (a * 4 + b) * depth + c

    every = [(a, c) for a in range(groups) for c in range(depth)]
    across = [(place(a, u, c), place(a, 3 - u, c)) for a, c in every for u in (1, 2)]
    along_x = [(place(a, u, c), place(1 - a, u, c)) for a, c in every for u in (1, 2)]
    along_z = [(place(a, u, c), place(a, u, c ^ 1)) for a, c in every for u in (1, 2)]
    inside = [(place(a, u, c), place(a, v, c)) for a, c in every for u, v in ((1, 0), (2, 3))]
    cores = [(place(a, u, c), place(a, u ^ 1, c)) for a, c in every for u in range(4)]
    chips = [(place(a, u, c), place(a, u ^ 2, c)) for a, c in every for u in range(4)]

    def plan(ranks, tallies, pick, scalars, lane0, lane1):
        g, t, d = (lax.axis_index(a) for a in AXES)
        q = 2 * g + (d & 1)
        middle, t0, t1, t2 = ranks[1], tallies[0], tallies[1], tallies[2]
        is_mid = (t == middle).astype(jnp.int32)
        crossing = jnp.where(middle == 2, half - t0, half - t2)
        def by_rank(first, low, high, last):
            return jnp.where(t == 0, first, jnp.where(t == 3, last, jnp.where(t == 1, low, high)))

        pick[0] = jnp.clip(crossing - fewest, 0, old_blocks - 2 - fewest)
        base = jnp.where(t == 1, (old_blocks - crossing) * BLOCK, 0)
        early, relay = split(crossing)
        lane0[0] = base
        lane1[0] = by_rank(0, 0, (old_blocks - most) * BLOCK, 0)

        values = [
            t,
            0,
            by_rank(old_blocks, is_mid * (half - t0), is_mid * (half - t2), old_blocks),
            by_rank(0, 0, crossing, t2 - old_blocks),
            by_rank(t0, is_mid * t1, is_mid * t1, t2),
            is_mid,
            by_rank(0, (half - t0) * BLOCK, 0, 0),
            q,
            by_rank(0, 0, 0, most - (t2 - old_blocks)),
            by_rank(t0 - old_blocks, 0, 0, t2 - old_blocks),
            by_rank(old_blocks, 0, 0, 0),
            by_rank(2 * old_blocks, 0, old_blocks - most, 2 * old_blocks),
            base + 2 * crossing * q * UNIT,
            base + (2 * crossing * q + early) * UNIT,
            base + (2 * crossing * (3 - q) + 2 * relay) * UNIT,
        ]
        values[1] = by_rank(0, is_mid * (t0 - old_blocks), 0, 0)
        for k, value in enumerate(values):
            scalars[k] = value

    smem = pl.BlockSpec(memory_space=pltpu.SMEM)
    one = jax.ShapeDtypeStruct((1,), jnp.int32)
    pick, scalars, lane0, lane1 = pl.pallas_call(
        plan,
        in_specs=[smem] * 2,
        out_specs=[smem] * 4,
        out_shape=(one, jax.ShapeDtypeStruct((15,), jnp.int32)) + (one,) * 2,
        name="plan",
    )(ranks, tallies)
    pick, lane0, lane1 = (a.reshape(()) for a in (pick, lane0, lane1))

    def permute(a, pairs):
        return lax.ppermute(a, AXES, pairs)

    tie = lax.optimization_barrier

    def body(v, args):
        scalars, lane0, lane1, x, z, dt, enter, leave, w, ssm, conv, *params = args
        early, relay = split(v)
        second_n = 2 * v - early
        n, k, m = early * UNIT, second_n * UNIT, relay * UNIT
        far_n = n + k - 2 * m

        first = cut_rows(scalars, w, n)
        y1 = permute(first, across)
        scalars, first = tie((scalars, first))
        out_w, side, second, third, partial, states = decode_here(
            scalars, cap, most, (k, far_n), x, z, dt, enter, leave, w, ssm, conv, *params
        )
        y2 = permute(second, across)
        y1, states, partial, side = tie((y1, states, partial, side))
        x1, z1 = permute(y1, along_x), permute(y1, along_z)

        features = partial.shape[1]
        odd = scalars[0] & 1
        core = odd * (features // 2)
        mine = lax.dynamic_slice_in_dim(partial, core, features // 2, 1)
        theirs = lax.dynamic_slice_in_dim(partial, features // 2 - core, features // 2, 1)
        chip_sum = (mine + permute(theirs, cores)).astype(BF)
        total = (chip_sum.astype(F32) + permute(chip_sum, chips).astype(F32)).astype(BF)
        across_s = permute(lax.dynamic_slice_in_dim(states, lane0, v * BLOCK, 1), across)
        side_s = permute(lax.dynamic_slice_in_dim(states, lane1, most * BLOCK, 1), inside)

        y2, x1, z1, side, third, total, across_s, side_s = tie(
            (y2, x1, z1, side, third, total, across_s, side_s)
        )

        y3 = permute(third, across)
        x2, z2 = permute(y2, along_x), permute(y2, along_z)
        side = permute(side, inside)
        to_x, to_z = z1[:m], x1[m : 2 * m]
        x3, z3 = permute(to_x, along_x), permute(to_z, along_z)
        scalars, to_x, to_z = tie((scalars, to_x, to_z))
        other = permute(total, cores)
        decoded = jnp.concatenate(
            [jnp.where(odd == 0, total, other), jnp.where(odd == 0, other, total)], axis=1
        )
        out_w = place_rows(
            scalars,
            out_w,
            [
                (y1, 0, n, lambda q: 2 * v * q),
                (y2, 0, k, lambda q: 2 * v * q + early),
                (x1, 0, n, lambda q: 2 * v * (q ^ 2)),
                (z1, 0, n, lambda q: 2 * v * (q ^ 1)),
            ],
            blanks=True,
        )
        new_ssm, new_conv = place_states(scalars, cap, states, side_s, across_s, ssm.shape[1])
        out_w = place_rows(
            scalars,
            out_w,
            [
                (x2, 0, k, lambda q: 2 * v * (q ^ 2) + early),
                (z2, 0, k, lambda q: 2 * v * (q ^ 1) + early),
            ],
            side,
        )
        out_w = place_rows(
            scalars,
            out_w,
            [
                (x3, 0, m, lambda q: 2 * v * (3 - q)),
                (z3, 0, m, lambda q: 2 * v * (3 - q) + relay),
                (y3, 0, far_n, lambda q: 2 * v * (3 - q) + 2 * relay),
            ],
        )
        return decoded, out_w, new_ssm, new_conv

    args = (scalars, lane0, lane1, x, z, dt, enter, leave, w, ssm, conv, logs, taps, offs, inc, res)
    branches = [lambda args, v=v: body(v, args) for v in range(fewest, old_blocks - 1)]
    decoded, out_w, new_ssm, new_conv = lax.switch(pick, branches, args)
    return decoded.reshape(x.shape[0], x.shape[1], -1), out_w, new_ssm, new_conv.T


def solution(mesh):
    placed = (
        P(None, ("groups", "dp"), "tp"),
        P(None, ("groups", "dp"), "tp"),
        P(None, ("groups", "dp"), "tp"),
        P(None, ("groups", "dp"), None),
        P(None, ("groups", "dp"), None),
        P("tp", None),
        P("tp", ("groups", "dp")),
        P("tp", ("groups", "dp")),
    ) + (P(),) * 7
    square = mesh.shape["tp"] == 4 and mesh.shape["groups"] == 2 and mesh.shape["dp"] % 2 == 0
    return jax.shard_map(
        neighbours if square else general,
        mesh=mesh,
        in_specs=placed,
        out_specs=(
            P(None, ("groups", "dp"), None),
            P(("groups", "tp"), None),
            P("tp", ("groups", "dp")),
            P("tp", ("groups", "dp")),
        ),
        check_vma=False,
    )
```

```python
import jax
import jax.numpy as jnp
from jax import lax
from jax.experimental import pallas as pl
from jax.experimental.pallas import tpu as pltpu
from jax.sharding import PartitionSpec as P

BLOCK = 128
UNIT = 16
BF = jnp.bfloat16
F32 = jnp.float32
AXES = ("groups", "tp", "dp")


def owner_ranges(remaining_ranks, holder_segment_tallies, holder_ranks):
    starts = jnp.cumsum(holder_segment_tallies) - holder_segment_tallies
    roster = jnp.arange(holder_ranks, dtype=jnp.int32)
    match = (remaining_ranks[None, :] == roster[:, None]).astype(jnp.int32)
    first = jnp.sum(match * starts[None, :], axis=1)
    total = jnp.sum(match * holder_segment_tallies[None, :], axis=1)
    return first, total


def pack_rows(columns, first, total, slot_rows):
    padded = jnp.pad(columns, ((0, slot_rows), (0, 0)))
    places = jnp.arange(slot_rows, dtype=jnp.int32)

    def one_owner(start, count):
        rows = lax.dynamic_slice_in_dim(padded, start * BLOCK, slot_rows, 0)
        return jnp.where((places < count * BLOCK)[:, None], rows, jnp.zeros_like(rows))

    packed = jax.vmap(one_owner)(first, total)
    return packed.reshape(-1, columns.shape[1])


def relocate_everywhere(rows, first, total, slot_rows):
    spread = lax.all_to_all(rows, "tp", split_axis=1, concat_axis=0, tiled=True)
    packed = pack_rows(spread, first, total, slot_rows)
    return lax.all_to_all(packed, "tp", split_axis=0, concat_axis=1, tiled=True)


def decode_plain(x, z, dt, enter, leave, ssm, conv, logs, taps, offs, inc, res, weights):
    steps, seqs, channels = x.shape
    h = ssm.reshape(channels, seqs, -1)
    window = conv.reshape(channels, seqs, 4)
    decay = -jnp.exp(logs)
    gated = []
    for step in range(steps):
        now = x[step].astype(F32).T
        window = jnp.concatenate([window[:, :, 1:], now[:, :, None]], axis=2)
        inner = jax.nn.silu(jnp.sum(window * taps[:, None, :], axis=2) + offs[:, None])
        delta = jax.nn.softplus(dt[step].astype(F32).T + inc[:, None])
        h = (
            jnp.exp(delta[:, :, None] * decay[:, None, :]) * h
            + (delta * inner)[:, :, None] * enter[step][None, :, :]
        )
        y = jnp.sum(h * leave[step][None, :, :], axis=2) + res[:, None] * inner
        gated.append((y * jax.nn.silu(z[step].astype(F32).T)).astype(BF))
    gated = jnp.concatenate(gated, axis=1)
    partial = lax.dot_general(
        gated, weights, (((0,), (0,)), ((), ())), preferred_element_type=F32
    )
    return partial, h.reshape(channels, -1), window.reshape(channels, -1)


def general(x, z, dt, enter, leave, w, ssm, conv, logs, taps, offs, inc, res, ranks, tallies):
    holders = lax.axis_size("tp")
    mine = lax.axis_index("tp")
    width, old = logs.shape[0], w.shape[0]
    slot_rows = (width // BLOCK // (holders * 3 // 4) + 2) * BLOCK
    first, total = owner_ranges(ranks, tallies, holders)

    def own(a):
        return lax.dynamic_slice_in_dim(a, mine * old, old, 0)

    moved_w = relocate_everywhere(w, first, total, slot_rows)
    partial, ssm, conv = decode_plain(
        x, z, dt, enter, leave, ssm, conv, own(logs), own(taps), own(offs), own(inc), own(res), w
    )
    decoded = lax.psum(partial, "tp").astype(BF).reshape(x.shape[0], x.shape[1], -1)
    return (
        decoded,
        moved_w,
        relocate_everywhere(ssm, first, total, slot_rows),
        relocate_everywhere(conv, first, total, slot_rows),
    )


def each(low, high, act):
    lax.fori_loop(low, high, lambda b, _: (act(b), 0)[1], 0)


CHUNK = 256
WIDE = 2048


def decode_kernel(
    sc, x, z, dt, enter, leave, h0, hist, logs, taps, offs, inc, res, w_all,
    out_w, side, second, third, partial, states, ys, deltas, feeds, turned, w, w_sem, own_sem, side_sem, cut_sem,
):
    i = pl.program_id(0)
    steps, seqs, chunk = x.shape
    latents = logs.shape[0]
    per = chunk // BLOCK
    blocks = w_all.shape[0] // BLOCK
    slots = out_w.shape[0] // BLOCK
    side_n = side.shape[0] // BLOCK
    own_src, own_n, own_dst, side_src = sc[1], sc[2], sc[3], sc[11]

    def rows(b):
        return pl.ds(pl.multiple_of(b * BLOCK, BLOCK), BLOCK)

    def fetch(b):
        return pltpu.make_async_copy(w_all.at[rows(b)], w.at[rows(b)], w_sem.at[b])

    def keep(b):
        at = jnp.clip(b - own_src + own_dst, 0, slots - 1)
        return pltpu.make_async_copy(w.at[rows(b)], out_w.at[rows(at)], own_sem.at[b])

    def pass_on(b):
        at = jnp.clip(b - side_src, 0, side_n - 1)
        return pltpu.make_async_copy(w.at[rows(b)], side.at[rows(at)], side_sem.at[b])

    @pl.when(i == 0)
    def _():
        each(0, blocks, lambda b: fetch(b).start())
        partial[...] = jnp.zeros_like(partial)

    decay = -jnp.exp(logs[...])
    xs = [x[t].astype(F32) for t in range(steps)]
    window = [hist[k] for k in range(1, 4)] + xs
    tap = [taps[k : k + 1, :] for k in range(4)]
    inners = []
    for t in range(steps):
        mixed = offs[...] + sum(window[t + k] * tap[k] for k in range(4))
        inner = mixed / (1.0 + jnp.exp(-mixed))
        v = dt[t].astype(F32) + inc[...]
        delta = jnp.maximum(v, 0.0) + jnp.log1p(jnp.exp(-jnp.abs(v)))
        inners.append(inner)
        deltas[t * seqs : (t + 1) * seqs, :] = delta
        feeds[t * seqs : (t + 1) * seqs, :] = delta * inner
    turned[...] = h0[...].T

    def wide(a):
        return jnp.concatenate([a] * per, axis=1)

    def sequence(s, _):
        at = pl.ds(pl.multiple_of(s * latents, latents), latents)
        h = turned[at, :]
        for t in range(steps):
            c = t * seqs + s
            row = pl.ds(c, 1)
            h = jnp.exp(deltas[row, :] * decay) * h + feeds[row, :] * wide(enter[c])
            ys[row, :] = jnp.sum(h * wide(leave[c]), axis=0, keepdims=True)
        states[at, :] = h.astype(BF)
        return 0

    lax.fori_loop(0, seqs, sequence, 0)
    states[seqs * latents :, :] = jnp.concatenate(xs, axis=0).astype(BF)
    gated = []
    for t in range(steps):
        y = ys[t * seqs : (t + 1) * seqs, :] + res[...] * inners[t]
        g = z[t].astype(F32)
        gated.append(y * (g / (1.0 + jnp.exp(-g))))
    gated = jnp.concatenate(gated, axis=0).astype(BF)

    def arrived(j, _):
        b = i * per + j
        fetch(b).wait()

        @pl.when((b >= own_src) & (b < own_src + own_n))
        def _():
            keep(b).start()

        @pl.when((b >= side_src) & (b < side_src + side_n))
        def _():
            pass_on(b).start()

        return 0

    lax.fori_loop(0, per, arrived, 0)
    last = i == pl.num_programs(0) - 1
    cuts = [
        pltpu.make_async_copy(
            w.at[pl.ds(pl.multiple_of(sc[row], UNIT), to.shape[0])], to, cut_sem.at[k]
        )
        for k, (row, to) in enumerate(((13, second), (14, third)))
    ]

    @pl.when(last)
    def _():
        for copy in cuts:
            copy.start()

    here = pl.ds(pl.multiple_of(i * chunk, chunk), chunk)

    def project(k):
        cols = pl.ds(pl.multiple_of(k * WIDE, WIDE), WIDE)
        partial[:, cols] += jnp.dot(gated, w[here, cols], preferred_element_type=F32)

    each(0, partial.shape[1] // WIDE, project)

    @pl.when(last)
    def _():
        for copy in cuts:
            copy.wait()
        each(own_src, own_src + own_n, lambda b: keep(b).wait())
        each(side_src, jnp.minimum(side_src + side_n, blocks), lambda b: pass_on(b).wait())


def decode_here(scalars, slots, side_n, cut_rows, x, z, dt, enter, leave, w, ssm, conv, logs, taps, offs, inc, res):
    steps, seqs, channels = x.shape
    latents = logs.shape[1]
    features = w.shape[1]
    n = channels // CHUNK
    series = pl.BlockSpec((steps, seqs, CHUNK), lambda i, sc: (0, 0, i))
    small = pl.BlockSpec((steps * seqs, latents, BLOCK), lambda i, sc: (0, 0, 0))

    def lanes(rows):
        return pl.BlockSpec((rows, CHUNK), lambda i, sc: (0, sc[0] * n + i))

    grid_spec = pltpu.PrefetchScalarGridSpec(
        num_scalar_prefetch=1,
        grid=(n,),
        in_specs=[
            series, series, series, small, small,
            pl.BlockSpec((CHUNK, seqs * latents), lambda i, sc: (i, 0)),
            pl.BlockSpec((4, seqs, CHUNK), lambda i, sc: (0, 0, i)),
            lanes(latents), lanes(4), lanes(1), lanes(1), lanes(1),
            pl.BlockSpec(memory_space=pltpu.HBM),
        ],
        out_specs=[
            pl.BlockSpec(memory_space=pltpu.HBM),
            pl.BlockSpec(memory_space=pltpu.HBM),
            pl.BlockSpec(memory_space=pltpu.HBM),
            pl.BlockSpec(memory_space=pltpu.HBM),
            pl.BlockSpec((steps * seqs, features), lambda i, sc: (0, 0)),
            pl.BlockSpec((seqs * (latents + 4), CHUNK), lambda i, sc: (0, i)),
        ],
        scratch_shapes=[
            pltpu.VMEM((steps * seqs, CHUNK), F32),
            pltpu.VMEM((steps * seqs, CHUNK), F32),
            pltpu.VMEM((steps * seqs, CHUNK), F32),
            pltpu.VMEM((seqs * latents, CHUNK), F32),
            pltpu.VMEM((channels, features), BF),
            pltpu.SemaphoreType.DMA((channels // BLOCK,)),
            pltpu.SemaphoreType.DMA((channels // BLOCK,)),
            pltpu.SemaphoreType.DMA((channels // BLOCK,)),
            pltpu.SemaphoreType.DMA((2,)),
        ],
    )
    rows = steps * seqs
    return pl.pallas_call(
        decode_kernel,
        grid_spec=grid_spec,
        out_shape=(
            jax.ShapeDtypeStruct((slots * BLOCK, features), BF),
            jax.ShapeDtypeStruct((side_n * BLOCK, features), BF),
            jax.ShapeDtypeStruct((cut_rows[0], features), BF),
            jax.ShapeDtypeStruct((cut_rows[1], features), BF),
            jax.ShapeDtypeStruct((rows, features), F32),
            jax.ShapeDtypeStruct((seqs * (latents + 4), channels), BF),
        ),
        compiler_params=pltpu.CompilerParams(vmem_limit_bytes=50 << 20),
        cost_estimate=HINT,
        name="decode",
    )(
        scalars, x, z, dt,
        jnp.broadcast_to(enter.reshape(rows, latents, 1), (rows, latents, BLOCK)),
        jnp.broadcast_to(leave.reshape(rows, latents, 1), (rows, latents, BLOCK)),
        ssm, conv.T.reshape(seqs, 4, channels).transpose(1, 0, 2), logs.T, taps.T,
        offs.reshape(1, -1), inc.reshape(1, -1), res.reshape(1, -1), w,
    )


HINT = pl.CostEstimate(flops=0, bytes_accessed=1024, transcendentals=0)


def cut_rows(scalars, w, rows):
    def kernel(sc, w_ref, out, sem):
        copy = pltpu.make_async_copy(
            w_ref.at[pl.ds(pl.multiple_of(sc[12], UNIT), rows)], out, sem
        )
        copy.start()
        copy.wait()

    return pl.pallas_call(
        kernel,
        grid_spec=pltpu.PrefetchScalarGridSpec(
            num_scalar_prefetch=1,
            grid=(),
            in_specs=[pl.BlockSpec(memory_space=pltpu.HBM)],
            out_specs=pl.BlockSpec(memory_space=pltpu.VMEM),
            scratch_shapes=[pltpu.SemaphoreType.DMA],
        ),
        out_shape=jax.ShapeDtypeStruct((rows, w.shape[1]), w.dtype),
        compiler_params=pltpu.CompilerParams(vmem_limit_bytes=8 << 20),
        cost_estimate=HINT,
        name="cut_rows",
    )(scalars, w)


def place_rows(scalars, out_w, pieces, side=None, blanks=False):
    slots, features = out_w.shape[0] // BLOCK, out_w.shape[1]
    arrays = []
    for piece in pieces:
        if not any(piece[0] is a for a in arrays):
            arrays.append(piece[0])
    jobs = []
    for array, first, rows, offset in pieces:
        jobs.append((next(k for k, a in enumerate(arrays) if a is array), first, rows, offset))
    side_n = 0 if side is None else side.shape[0] // BLOCK
    operands = arrays + ([] if side is None else [side])
    staged = sum(job[2] for job in jobs)

    def kernel(sc, *refs):
        ins, out = refs[: len(operands)], refs[len(operands) + 1]
        stage, side_stage, sems, side_sems, blank, blank_sems = refs[len(operands) + 2 :]
        recv, row0, q = sc[5], sc[6], sc[7]
        c_src, c_n, c_dst = sc[8], sc[9], sc[10]
        starts = [sum(job[2] for job in jobs[:k]) for k in range(len(jobs))]

        def fetch(k):
            which, first, rows, _ = jobs[k]
            return pltpu.make_async_copy(
                ins[which].at[pl.ds(first, rows)],
                stage.at[pl.ds(starts[k], rows)],
                sems.at[2 * k],
            )

        def store(k):
            _, _, rows, offset = jobs[k]
            row = jnp.clip(row0 + offset(q) * UNIT, 0, slots * BLOCK - rows)
            return pltpu.make_async_copy(
                stage.at[pl.ds(starts[k], rows)],
                out.at[pl.ds(pl.multiple_of(row, UNIT), rows)],
                sems.at[2 * k + 1],
            )

        def side_fetch(b):
            src = jnp.clip(c_src + b, 0, side_n - 1) * BLOCK
            return pltpu.make_async_copy(
                ins[-1].at[pl.ds(pl.multiple_of(src, BLOCK), BLOCK)],
                side_stage.at[pl.ds(pl.multiple_of(b * BLOCK, BLOCK), BLOCK)],
                side_sems.at[2 * b],
            )

        def side_store(b):
            dst = jnp.clip(c_dst + b, 0, slots - 1) * BLOCK
            return pltpu.make_async_copy(
                side_stage.at[pl.ds(pl.multiple_of(b * BLOCK, BLOCK), BLOCK)],
                out.at[pl.ds(pl.multiple_of(dst, BLOCK), BLOCK)],
                side_sems.at[2 * b + 1],
            )

        def clear(b):
            return pltpu.make_async_copy(
                blank, out.at[pl.ds(pl.multiple_of(b * BLOCK, BLOCK), BLOCK)], blank_sems.at[b]
            )

        if blanks:
            blank[...] = jnp.zeros_like(blank)
            each(sc[4], slots, lambda b: clear(b).start())

        @pl.when(recv == 1)
        def _():
            for k in range(len(jobs)):
                fetch(k).start()
            for k in range(len(jobs)):
                fetch(k).wait()
                store(k).start()
            for k in range(len(jobs)):
                store(k).wait()

        if side_n:
            count = jnp.minimum(c_n, side_n)
            each(0, count, lambda b: side_fetch(b).start())

            def pass_on(b):
                side_fetch(b).wait()
                side_store(b).start()

            each(0, count, pass_on)
            each(0, count, lambda b: side_store(b).wait())

        if blanks:
            each(sc[4], slots, lambda b: clear(b).wait())

    any_spec = pl.BlockSpec(memory_space=pl.ANY)
    side_rows = max(side_n * BLOCK, UNIT)
    return pl.pallas_call(
        kernel,
        grid_spec=pltpu.PrefetchScalarGridSpec(
            num_scalar_prefetch=1,
            grid=(),
            in_specs=[any_spec] * (len(operands) + 1),
            out_specs=any_spec,
            scratch_shapes=[
                pltpu.VMEM((staged, features), out_w.dtype),
                pltpu.VMEM((side_rows, features), out_w.dtype),
                pltpu.SemaphoreType.DMA((2 * len(jobs),)),
                pltpu.SemaphoreType.DMA((2 * max(side_n, 1),)),
                pltpu.VMEM((BLOCK if blanks else UNIT, features), out_w.dtype),
                pltpu.SemaphoreType.DMA((slots,)),
            ],
        ),
        out_shape=jax.ShapeDtypeStruct(out_w.shape, out_w.dtype),
        input_output_aliases={len(operands) + 1: 0},
        compiler_params=pltpu.CompilerParams(
            vmem_limit_bytes=(staged + side_rows + BLOCK) * features * 2 + (2 << 20)
        ),
        cost_estimate=HINT,
        name="place_rows",
    )(scalars, *operands, out_w)


def place_states(scalars, slots, own, side, across, latent_rows):
    rows = own.shape[0]
    seqs = (rows - latent_rows) // 4

    def kernel(sc, own_ref, side_ref, across_ref, ssm, conv, turned):
        own_src, own_n, own_dst, filled = sc[1], sc[2], sc[3], sc[4]
        recv, recv_dst = sc[5], sc[6] // BLOCK
        c_src, c_n, c_dst = sc[8], sc[9], sc[10]

        def rows_of(b):
            return pl.ds(pl.multiple_of(b * BLOCK, BLOCK), BLOCK)

        def put(b, ref, at):
            block = ref[:, rows_of(at)].astype(F32)
            ssm[rows_of(b), :] = block[:latent_rows].T
            for k in range(4):
                at = latent_rows + k * seqs
                turned[pl.ds(k, seqs, stride=4), :] = block[at : at + seqs]
            conv[:, rows_of(b)] = turned[...]

        across_n = across_ref.shape[1] // BLOCK

        def empty(b):
            ssm[rows_of(b), :] = jnp.zeros((BLOCK, latent_rows), F32)
            conv[:, rows_of(b)] = jnp.zeros((rows - latent_rows, BLOCK), F32)

        first = jnp.where(recv == 1, recv_dst, 0)
        count = jnp.where(recv == 1, across_n, 0)
        each(own_dst, own_dst + own_n, lambda b: put(b, own_ref, b - own_dst + own_src))
        each(c_dst, c_dst + c_n, lambda b: put(b, side_ref, b - c_dst + c_src))
        each(first, first + count, lambda b: put(b, across_ref, b - recv_dst))
        each(filled, slots, empty)

    vmem = pl.BlockSpec(memory_space=pltpu.VMEM)
    return pl.pallas_call(
        kernel,
        grid_spec=pltpu.PrefetchScalarGridSpec(
            num_scalar_prefetch=1,
            grid=(),
            in_specs=[vmem] * 3,
            out_specs=[vmem] * 2,
            scratch_shapes=[pltpu.VMEM((rows - latent_rows, BLOCK), F32)],
        ),
        out_shape=(
            jax.ShapeDtypeStruct((slots * BLOCK, latent_rows), F32),
            jax.ShapeDtypeStruct((rows - latent_rows, slots * BLOCK), F32),
        ),
        compiler_params=pltpu.CompilerParams(vmem_limit_bytes=24 << 20),
        cost_estimate=HINT,
        name="place_states",
    )(scalars, own, side, across)


def split(blocks):
    return blocks, (2 * blocks + 5) // 11


def neighbours(x, z, dt, enter, leave, w, ssm, conv, logs, taps, offs, inc, res, ranks, tallies):
    groups, depth = lax.axis_size("groups"), lax.axis_size("dp")
    old_blocks = w.shape[0] // BLOCK
    cap = (logs.shape[0] // BLOCK) // 3 + 2
    most = cap - old_blocks
    half = 2 * old_blocks
    fewest = half - cap

    def place(a, b, c):
        return (a * 4 + b) * depth + c

    every = [(a, c) for a in range(groups) for c in range(depth)]
    across = [(place(a, u, c), place(a, 3 - u, c)) for a, c in every for u in (1, 2)]
    along_x = [(place(a, u, c), place(1 - a, u, c)) for a, c in every for u in (1, 2)]
    along_z = [(place(a, u, c), place(a, u, c ^ 1)) for a, c in every for u in (1, 2)]
    inside = [(place(a, u, c), place(a, v, c)) for a, c in every for u, v in ((1, 0), (2, 3))]
    cores = [(place(a, u, c), place(a, u ^ 1, c)) for a, c in every for u in range(4)]
    chips = [(place(a, u, c), place(a, u ^ 2, c)) for a, c in every for u in range(4)]

    def plan(ranks, tallies, pick, scalars, lane0, lane1):
        g, t, d = (lax.axis_index(a) for a in AXES)
        q = 2 * g + (d & 1)
        middle, t0, t1, t2 = ranks[1], tallies[0], tallies[1], tallies[2]
        is_mid = (t == middle).astype(jnp.int32)
        crossing = jnp.where(middle == 2, half - t0, half - t2)
        def by_rank(first, low, high, last):
            return jnp.where(t == 0, first, jnp.where(t == 3, last, jnp.where(t == 1, low, high)))

        pick[0] = jnp.clip(crossing - fewest, 0, old_blocks - 2 - fewest)
        base = jnp.where(t == 1, (old_blocks - crossing) * BLOCK, 0)
        early, relay = split(crossing)
        lane0[0] = base
        lane1[0] = by_rank(0, 0, (old_blocks - most) * BLOCK, 0)

        values = [
            t,
            0,
            by_rank(old_blocks, is_mid * (half - t0), is_mid * (half - t2), old_blocks),
            by_rank(0, 0, crossing, t2 - old_blocks),
            by_rank(t0, is_mid * t1, is_mid * t1, t2),
            is_mid,
            by_rank(0, (half - t0) * BLOCK, 0, 0),
            q,
            by_rank(0, 0, 0, most - (t2 - old_blocks)),
            by_rank(t0 - old_blocks, 0, 0, t2 - old_blocks),
            by_rank(old_blocks, 0, 0, 0),
            by_rank(2 * old_blocks, 0, old_blocks - most, 2 * old_blocks),
            base + 2 * crossing * q * UNIT,
            base + (2 * crossing * q + early) * UNIT,
            base + (2 * crossing * (3 - q) + 2 * relay) * UNIT,
        ]
        values[1] = by_rank(0, is_mid * (t0 - old_blocks), 0, 0)
        for k, value in enumerate(values):
            scalars[k] = value

    smem = pl.BlockSpec(memory_space=pltpu.SMEM)
    one = jax.ShapeDtypeStruct((1,), jnp.int32)
    pick, scalars, lane0, lane1 = pl.pallas_call(
        plan,
        in_specs=[smem] * 2,
        out_specs=[smem] * 4,
        out_shape=(one, jax.ShapeDtypeStruct((15,), jnp.int32)) + (one,) * 2,
        name="plan",
    )(ranks, tallies)
    pick, lane0, lane1 = (a.reshape(()) for a in (pick, lane0, lane1))

    def permute(a, pairs):
        return lax.ppermute(a, AXES, pairs)

    tie = lax.optimization_barrier

    def body(v, args):
        scalars, lane0, lane1, x, z, dt, enter, leave, w, ssm, conv, *params = args
        early, relay = split(v)
        second_n = 2 * v - early
        n, k, m = early * UNIT, second_n * UNIT, relay * UNIT
        far_n = n + k - 2 * m

        first = cut_rows(scalars, w, n)
        y1 = permute(first, across)
        scalars, first = tie((scalars, first))
        out_w, side, second, third, partial, states = decode_here(
            scalars, cap, most, (k, far_n), x, z, dt, enter, leave, w, ssm, conv, *params
        )
        y2 = permute(second, across)
        y1, states, partial, side = tie((y1, states, partial, side))
        x1, z1 = permute(y1, along_x), permute(y1, along_z)

        features = partial.shape[1]
        odd = scalars[0] & 1
        core = odd * (features // 2)
        mine = lax.dynamic_slice_in_dim(partial, core, features // 2, 1)
        theirs = lax.dynamic_slice_in_dim(partial, features // 2 - core, features // 2, 1)
        chip_sum = (mine + permute(theirs, cores)).astype(BF)
        total = (chip_sum.astype(F32) + permute(chip_sum, chips).astype(F32)).astype(BF)
        across_s = permute(lax.dynamic_slice_in_dim(states, lane0, v * BLOCK, 1), across)
        side_s = permute(lax.dynamic_slice_in_dim(states, lane1, most * BLOCK, 1), inside)

        y2, x1, z1, side, third, total, across_s, side_s = tie(
            (y2, x1, z1, side, third, total, across_s, side_s)
        )

        y3 = permute(third, across)
        x2, z2 = permute(y2, along_x), permute(y2, along_z)
        side = permute(side, inside)
        to_x, to_z = z1[:m], x1[m : 2 * m]
        x3, z3 = permute(to_x, along_x), permute(to_z, along_z)
        scalars, to_x, to_z = tie((scalars, to_x, to_z))
        other = permute(total, cores)
        decoded = jnp.concatenate(
            [jnp.where(odd == 0, total, other), jnp.where(odd == 0, other, total)], axis=1
        )
        out_w = place_rows(
            scalars,
            out_w,
            [
                (y1, 0, n, lambda q: 2 * v * q),
                (y2, 0, k, lambda q: 2 * v * q + early),
                (x1, 0, n, lambda q: 2 * v * (q ^ 2)),
                (z1, 0, n, lambda q: 2 * v * (q ^ 1)),
            ],
            blanks=True,
        )
        new_ssm, new_conv = place_states(scalars, cap, states, side_s, across_s, ssm.shape[1])
        out_w = place_rows(
            scalars,
            out_w,
            [
                (x2, 0, k, lambda q: 2 * v * (q ^ 2) + early),
                (z2, 0, k, lambda q: 2 * v * (q ^ 1) + early),
            ],
            side,
        )
        out_w = place_rows(
            scalars,
            out_w,
            [
                (x3, 0, m, lambda q: 2 * v * (3 - q)),
                (z3, 0, m, lambda q: 2 * v * (3 - q) + relay),
                (y3, 0, far_n, lambda q: 2 * v * (3 - q) + 2 * relay),
            ],
        )
        return decoded, out_w, new_ssm, new_conv

    args = (scalars, lane0, lane1, x, z, dt, enter, leave, w, ssm, conv, logs, taps, offs, inc, res)
    branches = [lambda args, v=v: body(v, args) for v in range(fewest, old_blocks - 1)]
    decoded, out_w, new_ssm, new_conv = lax.switch(pick, branches, args)
    return decoded.reshape(x.shape[0], x.shape[1], -1), out_w, new_ssm, new_conv.T


def solution(mesh):
    placed = (
        P(None, ("groups", "dp"), "tp"),
        P(None, ("groups", "dp"), "tp"),
        P(None, ("groups", "dp"), "tp"),
        P(None, ("groups", "dp"), None),
        P(None, ("groups", "dp"), None),
        P("tp", None),
        P("tp", ("groups", "dp")),
        P("tp", ("groups", "dp")),
    ) + (P(),) * 7
    square = mesh.shape["tp"] == 4 and mesh.shape["groups"] == 2 and mesh.shape["dp"] % 2 == 0
    return jax.shard_map(
        neighbours if square else general,
        mesh=mesh,
        in_specs=placed,
        out_specs=(
            P(None, ("groups", "dp"), None),
            P(("groups", "tp"), None),
            P("tp", ("groups", "dp")),
            P("tp", ("groups", "dp")),
        ),
        check_vma=False,
    )
```
